512 devices in a mesh: attn: 4 (over x), tp: 8 (over y, core), exp: 16 (over z).
Axes of the slice: x: 4, y: 4, z: 16, core: 2. Of those that a mesh axis runs over, the one named last changes fastest.
Arguments:
- queries: bfloat16 [64, 6144], P(('attn', 'exp'), 'tp'), may hold values from -6 to 6
- cache_keys: bfloat16 [64, 512, 1024], P(('attn', 'exp'), None, 'tp'), may hold values from -6 to 6
- cache_values: bfloat16 [64, 512, 1024], P(('attn', 'exp'), None, 'tp'), may hold values from -6 to 6
- new_keys: bfloat16 [64, 1024], P(('attn', 'exp'), 'tp'), may hold values from -6 to 6
- new_values: bfloat16 [64, 1024], P(('attn', 'exp'), 'tp'), may hold values from -6 to 6
- lengths: int32 [64], P(('attn', 'exp')), may hold values from 1 to 512, 16384 in all
- moe_input: bfloat16 [1024, 3072], P(('attn', 'exp'), 'tp'), may hold values from -6 to 6
- router_weight: bfloat16 [8, 3072], P(None, 'tp'), may hold values from -0.109375 to 0.109375
- expert_ids: int32 [1024, 2], P(('attn', 'exp')), may hold values from 0 to 7, all different within a row; in each aligned block of 16 rows (0 to 15, 16 to 31, ...) at most 5 rows name the same one
- gate_weight: bfloat16 [16, 3072, 8192], P('exp', None, ('attn', 'tp')), may hold values from -0.109375 to 0.109375
- up_weight: bfloat16 [16, 3072, 8192], P('exp', None, ('attn', 'tp')), may hold values from -0.109375 to 0.109375
- down_weight: bfloat16 [16, 8192, 3072], P('exp', ('attn', 'tp')), may hold values from -0.09375 to 0.09375
Outputs:
- attention_out: bfloat16 [64, 6144], P(('attn', 'exp'), 'tp')
- expert_out: bfloat16 [1024, 3072], P(('attn', 'exp'), 'tp')
The draws below stay inside these ranges and needn't reach their ends.
Inputs may be any that keep to these rules, and one draw needn't show every extreme that they name: `expert_ids`: each row names two different experts. Among the rows of one device (aligned blocks of 16 rows) no expert is named more than 5 times, and some block names one expert exactly 5 times. `lengths`: some row has exactly 512 cached positions.
All inputs are finite; a program needn't handle non-finite values. No bound on the sum of `lengths` on one device may be relied on, other than what follows from the above.
Results may differ from the reference program's by a relative error of at most 0.02.
Values may be sent and summed in bfloat16 or wider, within the bound.
A program may use at most 64 MiB of HBM per device.

```python
import math
import jax
import jax.numpy as jnp
import numpy as np
from jax import lax

D = 3072
FF = 16384
EXPERTS = 8
HQ = 48
KVH = 8
HD = 128
RB_DEV = 16
CACHE = 512
HALVES = 16
CAP = 5
HGROUP = 256
ROWS_A = 64
ROWS_B = 1024


def draw_queries(key, part):
    base_key = jax.random.fold_in(key, 11)
    values = jnp.clip(jax.random.normal(base_key, (ROWS_A, HQ * HD), jnp.float32), -6.0, 6.0)
    return values.astype(jnp.bfloat16)


def draw_cache_keys(key, part):
    base_key = jax.random.fold_in(key, 12)
    values = jnp.clip(jax.random.normal(base_key, (ROWS_A, CACHE, KVH * HD), jnp.float32), -6.0, 6.0)
    return values.astype(jnp.bfloat16)


def draw_new_keys(key, part):
    base_key = jax.random.fold_in(key, 13)
    values = jnp.clip(jax.random.normal(base_key, (ROWS_A, KVH * HD), jnp.float32), -6.0, 6.0)
    return values.astype(jnp.bfloat16)


def spiked(drawn, rng, source, target, blocks, factor):
    owner, partner = [(jnp.arange(drawn.shape[dim]) // (drawn.shape[dim] // blocks)).reshape([-1 if axis == dim else 1 for axis in range(drawn.ndim)]) for dim in (source, target)]
    chosen = jax.random.permutation(rng, blocks)[partner]
    strong = (owner == chosen) | (owner == (partner + blocks // 2) % blocks)
    return jnp.where(strong, factor * drawn, drawn)


def block_levels(key, extent, cuts, smallest, top_value):
    def one(dim, shards_of):
        draws = jax.random.uniform(jax.random.fold_in(jax.random.fold_in(key, 6), dim), (shards_of,), jnp.float32, smallest / len(cuts), top_value / len(cuts))
        return jnp.repeat(jnp.exp(draws), extent[dim] // shards_of).reshape((-1,) + (1,) * (len(extent) - dim - 1))

    factor_of = one(*cuts[0])
    for cut in cuts[1:]:
        factor_of = factor_of * one(*cut)
    return factor_of


def split_up(amount, total, most, slope):
    loads = [(1 << 20) // math.isqrt(standing ** slope) + 1 for standing in range(2, amount + 1)]
    surplus, counts = total - most - (amount - 1), [1] * (amount - 1)
    while surplus > 0:
        free = [i for i in range(amount - 1) if counts[i] < most]
        pool, left = sum([loads[i] for i in free]), surplus
        for i in free:
            addition = min(most - counts[i], max(1, left * loads[i] // pool), surplus)
            counts[i] = counts[i] + addition
            surplus = surplus - addition
    return np.array([most] + counts)


def ragged_sizes(key, amount, total, most, skew):
    if amount == 2:
        one = jax.random.randint(key, (), max(1, total - most), min(most, total - 1) + 1)
        return jnp.stack([one, total - one])
    sizes = jnp.asarray(split_up(amount, total, most, skew), jnp.int32)
    pairs = (amount - 1) // 2
    donor, receiver = sizes[1:1 + 2 * pairs:2], sizes[2:2 + 2 * pairs:2]
    slack = jnp.minimum(donor - 1, most - receiver)
    moved = jax.random.randint(jax.random.fold_in(key, 1), (pairs,), 0, 1 << 20) % (slack + 1)
    sizes = sizes.at[1:1 + 2 * pairs:2].set(donor - moved).at[2:2 + 2 * pairs:2].set(receiver + moved)
    return sizes[jax.random.permutation(jax.random.fold_in(key, 2), amount)]


def deal_out(stream_key, own, number, rows, amount, top, bound, slope):
    sequence = jax.random.permutation(stream_key, amount)
    packed, common = shares(amount, rows * top, bound, slope, True), shares(amount, rows * top, bound, slope, False)
    places = jnp.arange(amount)

    def named(sizes, rotation):
        used = int((sizes > 0).sum())
        fixed = max(1, used // 4)
        passed = fixed + (places - fixed + rotation * (used - fixed)) % max(1, amount - fixed)
        return jnp.zeros((amount,), jnp.int32).at[sequence[jnp.where(places < fixed, places, passed)]].set(jnp.asarray(sizes, jnp.int32))

    sizes = jnp.where(number % 4 == 0, named(packed, number // 4), named(common, number - number // 4 - 1))
    mixed = jax.random.permutation(jax.random.fold_in(own, 3), amount)
    donor, taker = mixed[0:amount // 2 * 2:2], mixed[1:amount // 2 * 2:2]
    slack = jnp.minimum(sizes[donor] - 1, bound - sizes[taker]) // 2
    slack = jnp.where((donor == sequence[0]) | (taker == sequence[0]) | (sizes[taker] == 0), 0, jnp.maximum(slack, 0))
    passed = jax.random.randint(jax.random.fold_in(own, 4), (amount // 2,), 0, 1 << 20) % (slack + 1)
    sizes = sizes.at[donor].add(-passed).at[taker].add(passed)
    items = jnp.searchsorted(jnp.cumsum(sizes), jnp.arange(rows * top), side="right").astype(jnp.int32)
    grid = items.reshape(top, rows).T
    grid = grid[jax.random.permutation(jax.random.fold_in(own, 1), rows)]
    rotation = jax.random.randint(jax.random.fold_in(own, 2), (rows, 1), 0, top)
    return jnp.take_along_axis(grid, (jnp.arange(top)[None, :] + rotation) % top, axis=1)


def shares(number_of, total, most, skew, full):
    loads = [(1 << 20) // math.isqrt(standing ** skew) + 1 for standing in range(1, number_of + 1)]
    largest = most if full else min(most, max(-(-total // number_of), total * loads[0] // sum(loads)))
    least = 1 if total - largest >= number_of - 1 else 0
    given, spare = [largest] + [least] * (number_of - 1), total - largest - least * (number_of - 1)
    while spare > 0:
        movable = [i for i in range(1, number_of) if given[i] < largest] or [i for i in range(1, number_of) if given[i] < most]
        mass, remaining = sum([loads[i] for i in movable]), spare
        for i in movable:
            extra = min(most - given[i], max(1, remaining * loads[i] // mass), spare)
            given[i] = given[i] + extra
            spare = spare - extra
    return np.array(given)


def bell_draw(stream_key, extent, scale, most, cuts=(), kind=jnp.bfloat16):
    factor_of = block_levels(stream_key, extent, cuts, -0.22, 0.18) if cuts else 1.0
    entries = jax.random.normal(stream_key, extent, jnp.float32) * scale * factor_of
    return jnp.minimum(jnp.maximum(entries, -most), most).astype(kind)


def bell_draw_with(stream_key, shape, deviation, bound, pieces, heavy, held_as=jnp.bfloat16):
    drawn = deviation * jax.random.normal(stream_key, shape, jnp.float32)
    if pieces:
        drawn = drawn * block_levels(stream_key, shape, pieces, -0.22, 0.18)
    return jnp.clip(spiked(drawn, jax.random.fold_in(stream_key, 3), *heavy), -bound, bound).astype(held_as)


def setup_inputs(seed: int = 0) -> dict:
    arg_keys = jax.random.split(jax.random.key(seed), 13)
    queries = draw_queries(jax.random.fold_in(arg_keys[12], 71), 0)
    cache_keys = draw_cache_keys(jax.random.fold_in(arg_keys[12], 71), 0)
    cache_values = bell_draw(arg_keys[2], (ROWS_A, CACHE, KVH * HD), 1.0, 6.0, ((0, 64), (2, 8)))
    new_keys = draw_new_keys(jax.random.fold_in(arg_keys[12], 71), 0)
    new_values = bell_draw(arg_keys[4], (ROWS_A, KVH * HD), 1.0, 6.0, ((0, 64), (1, 8)))
    lengths = ragged_sizes(arg_keys[5], ROWS_A, ROWS_A * CACHE // 2, CACHE, 2).astype(jnp.int32)
    moe_input = bell_draw(arg_keys[6], (ROWS_B, D), 1.0, 6.0, ((0, 64), (1, 8)))
    router_weight = bell_draw(arg_keys[7], (EXPERTS, D), D ** -0.5, 0.109375, ((1, 8),))
    expert_ids_keys = jax.random.split(jax.random.fold_in(arg_keys[8], 1), ROWS_B // RB_DEV)
    expert_ids_turns = jax.random.permutation(jax.random.fold_in(arg_keys[8], 3), ROWS_B // RB_DEV)
    expert_ids = jax.vmap(lambda own, number: deal_out(jax.random.fold_in(arg_keys[8], 2), own, number, RB_DEV, EXPERTS, 2, CAP, 2))(expert_ids_keys, expert_ids_turns).reshape((ROWS_B, 2))
    gate_weight = bell_draw(arg_keys[9], (HALVES, D, FF // 2), D ** -0.5, 0.109375, ((0, 16), (2, 32)))
    up_weight = bell_draw(arg_keys[10], (HALVES, D, FF // 2), D ** -0.5, 0.109375, ((0, 16), (2, 32)))
    down_weight = bell_draw_with(arg_keys[11], (HALVES, FF // 2, D), FF ** -0.5, 0.09375, ((0, 16), (1, 32)), (1, 2, 32, 2.75))
    return {"queries": queries, "cache_keys": cache_keys, "cache_values": cache_values, "new_keys": new_keys, "new_values": new_values, "lengths": lengths, "moe_input": moe_input, "router_weight": router_weight, "expert_ids": expert_ids, "gate_weight": gate_weight, "up_weight": up_weight, "down_weight": down_weight}


def attention_core(queries, cache_keys, cache_values, new_keys, new_values, lengths):
    row_count = queries.shape[0]
    per_key = HQ // KVH
    score_scale = 1.0 / math.sqrt(HD)
    query_heads = queries.astype(jnp.float32).reshape(row_count, KVH, per_key, HD)
    key_heads = cache_keys.astype(jnp.float32).reshape(row_count, CACHE, KVH, HD)
    value_heads = cache_values.astype(jnp.float32).reshape(row_count, CACHE, KVH, HD)
    own_keys = new_keys.astype(jnp.float32).reshape(row_count, KVH, HD)
    own_values = new_values.astype(jnp.float32).reshape(row_count, KVH, HD)
    scores = jnp.einsum('rhgd,rphd->rhgp', query_heads, key_heads) * score_scale
    own_score = jnp.einsum('rhgd,rhd->rhg', query_heads, own_keys) * score_scale
    visible = jnp.arange(CACHE, dtype=jnp.int32)[None, :] < lengths[:, None]
    scores = jnp.where(visible[:, None, None, :], scores, -jnp.inf)
    peak = jnp.maximum(lax.optimization_barrier(jnp.max(scores, axis=-1)), own_score)
    weights = jnp.exp(scores - peak[..., None])
    own_weight = jnp.exp(own_score - peak)
    total = lax.optimization_barrier(jnp.sum(weights, axis=-1)) + own_weight
    weights_bf = lax.optimization_barrier((weights / total[..., None]).astype(jnp.bfloat16)).astype(jnp.float32)
    own_bf = lax.optimization_barrier((own_weight / total).astype(jnp.bfloat16)).astype(jnp.float32)
    result = jnp.einsum('rhgp,rphd->rhgd', weights_bf, value_heads)
    result = result + own_bf[..., None] * own_values[:, :, None, :]
    return result.reshape(row_count, HQ * HD).astype(jnp.bfloat16)

def slot_numbers(expert_ids):
    flat_ids = expert_ids.reshape(-1)
    onehot = (flat_ids[:, None] == jnp.arange(EXPERTS, dtype=jnp.int32)[None, :]).astype(jnp.int32)
    before = jnp.cumsum(onehot, axis=0) - onehot
    return lax.optimization_barrier(jnp.sum(before * onehot, axis=1)).reshape(expert_ids.shape).astype(jnp.int32)

def expert_layer(moe_input, router_weight, expert_ids, gate_weight, up_weight, down_weight):
    blocks = ROWS_B // RB_DEV
    slot_ids = jax.vmap(slot_numbers)(expert_ids.reshape(blocks, RB_DEV, 2)).reshape(ROWS_B, 2)
    owner_row = (jnp.arange(ROWS_B, dtype=jnp.int32) // RB_DEV)[:, None]
    position = (owner_row * CAP + slot_ids).astype(jnp.int32)
    buffers = jnp.zeros((EXPERTS, blocks * CAP, D), moe_input.dtype)
    buffers = buffers.at[expert_ids, position].set(jnp.broadcast_to(moe_input[:, None, :], (ROWS_B, 2, D)))
    group_count = FF // HGROUP

    def one_expert(expert_index):
        row_tile_block = buffers[expert_index].astype(jnp.float32)
        start = (2 * expert_index).astype(jnp.int32)
        gate_pair = lax.dynamic_slice_in_dim(gate_weight, start, 2, 0).astype(jnp.float32)
        up_pair = lax.dynamic_slice_in_dim(up_weight, start, 2, 0).astype(jnp.float32)
        down_pair = lax.dynamic_slice_in_dim(down_weight, start, 2, 0).astype(jnp.float32)
        gate_sum = jnp.einsum('td,sdf->tsf', row_tile_block, gate_pair)
        up_sum = jnp.einsum('td,sdf->tsf', row_tile_block, up_pair)
        hidden_act = lax.optimization_barrier((jax.nn.silu(gate_sum) * up_sum).astype(jnp.bfloat16)).astype(jnp.float32)
        hidden_act = hidden_act.reshape(row_tile_block.shape[0], 2, group_count // 2, HGROUP)
        down_groups = down_pair.reshape(2, group_count // 2, HGROUP, D)
        down_terms = jnp.einsum('tsgf,sgfd->tsgd', hidden_act, down_groups)
        down_terms = lax.optimization_barrier(down_terms.astype(jnp.bfloat16)).astype(jnp.float32)
        return lax.optimization_barrier(jnp.sum(down_terms, axis=(1, 2)))
    outputs = lax.map(one_expert, jnp.arange(EXPERTS, dtype=jnp.int32))
    logits = jnp.einsum('rd,ed->re', moe_input.astype(jnp.float32), router_weight.astype(jnp.float32))
    chosen = jnp.take_along_axis(logits, expert_ids, axis=1)
    mixing = jax.nn.sigmoid(chosen - chosen[:, ::-1])
    selected_experts = outputs[expert_ids, position]
    return lax.optimization_barrier(jnp.sum(mixing[..., None] * selected_experts, axis=1)).astype(jnp.bfloat16)

def reference(queries, cache_keys, cache_values, new_keys, new_values, lengths, moe_input, router_weight, expert_ids, gate_weight, up_weight, down_weight):
    attention_out = attention_core(queries, cache_keys, cache_values, new_keys, new_values, lengths)
    expert_out = expert_layer(moe_input, router_weight, expert_ids, gate_weight, up_weight, down_weight)
    return (attention_out, expert_out)
```

```python
import math

import jax
import jax.numpy as jnp
from jax import lax
from jax.experimental import pallas as pl
from jax.experimental.pallas import tpu as pltpu
from jax.sharding import PartitionSpec as P

MESH = pl.DeviceIdType.MESH
BF = jnp.bfloat16
F32 = jnp.float32
CAP = 5
NX, NY, NZ, NT = 4, 4, 16, 8
W = 384
SLOTROWS = 80
HID = 256
D = 3072


def iota(shape, dim):
    return lax.broadcasted_iota(jnp.int32, shape, dim)


def chunk_of(m):
    return (m >= 5).astype(jnp.int32) + (m >= 10).astype(jnp.int32) + (m >= 15).astype(jnp.int32)


def dot(a, b):
    return jnp.dot(a, b, preferred_element_type=F32)


def drain(ref, sem):
    pltpu.make_async_copy(ref, ref, sem).wait()


def attention(q_ref, ck, cv, nk_ref, nv_ref, len_ref, att_ref):
    scale = 1.0 / math.sqrt(128)
    q = q_ref[...]
    heads = [q[:, h * 128 : (h + 1) * 128] for h in range(6)]
    qh = jnp.concatenate(heads + [jnp.zeros((2, 128), BF)], axis=0)
    scores = lax.dot_general(qh, ck[...], (((1,), (1,)), ((), ())), preferred_element_type=F32) * scale
    own = jnp.sum(qh.astype(F32) * nk_ref[...].astype(F32), axis=1, keepdims=True) * scale
    visible = iota(scores.shape, 1) < len_ref[...]
    scores = jnp.where(visible, scores, -jnp.inf)
    peak = jnp.maximum(jnp.max(scores, axis=1, keepdims=True), own)
    weights = jnp.exp(scores - peak)
    own_weight = jnp.exp(own - peak)
    total = jnp.sum(weights, axis=1, keepdims=True) + own_weight
    probs = (weights / total).astype(BF)
    own_prob = (own_weight / total).astype(BF).astype(F32)
    result = dot(probs, cv[...]) + own_prob * nv_ref[...].astype(F32)
    result = result.astype(BF)
    for h in range(6):
        att_ref[:, h * 128 : (h + 1) * 128] = result[h : h + 1, :]


def kernel(
    q_hbm, ck_hbm, cv_hbm, nk_hbm, nv_hbm, len_hbm, x_hbm, rw_hbm, ids_hbm, gate_hbm, up_hbm, down_hbm,
    att_ref, out_ref,
    q_ref, nk_ref, nv_ref, len_ref, x_ref, rw_ref, ids_ref, ck, cv, wg, wu, wd, pk, ra, ga, lhs, accg, accu, hid, sb, rb, pe, rc, lp, lr,
    small_sem, loc_sem, wsend, wrecv, asend, arecv, gsend, grecv, rsend, rrecv, esend, erecv, lsend, lrecv,
):
    x = lax.axis_index("attn")
    t = lax.axis_index("tp")
    z = lax.axis_index("exp")
    y = t // 2
    c = t % 2
    half = z % 2
    zi = z // 2
    same = half == c

    def dev(xx, tt, zz):
        return (xx, tt, zz)

    def start(src, dst, ssem, rsem, device):
        pltpu.make_async_remote_copy(
            src_ref=src, dst_ref=dst, send_sem=ssem, recv_sem=rsem, device_id=device, device_id_type=MESH
        ).start()

    small = [
        pltpu.make_async_copy(src, dst, small_sem.at[i])
        for i, (src, dst) in enumerate([
            (ids_hbm, ids_ref), (x_hbm, x_ref), (rw_hbm, rw_ref), (q_hbm, q_ref),
            (nk_hbm, nk_ref), (nv_hbm, nv_ref), (len_hbm, len_ref),
        ])
    ]
    for copy in small:
        copy.start()
    locals_ = [
        pltpu.make_async_copy(ck_hbm.at[0], ck, loc_sem.at[0]),
        pltpu.make_async_copy(cv_hbm.at[0], cv, loc_sem.at[1]),
        pltpu.make_async_copy(gate_hbm.at[0], wg.at[0], loc_sem.at[2]),
        pltpu.make_async_copy(up_hbm.at[0], wu.at[0], loc_sem.at[3]),
        pltpu.make_async_copy(down_hbm.at[0], wd.at[pl.ds(0, HID)], loc_sem.at[4]),
    ]

    barrier = pltpu.get_barrier_semaphore()

    def greet(device):
        pl.semaphore_signal(barrier, inc=1, device_id=device, device_id_type=MESH)

    for d in range(8):
        zs = 2 * ((zi + d) % 8) + c
        greet(dev(x, 2 * y + 1 - c, zs))
        if d:
            greet(dev(x, t, zs))
    @pl.when(jnp.logical_not(same))
    def _():
        greet(dev(x, t, 2 * zi + c))

    for dt in range(1, NT):
        greet(dev(x, (t + dt) % NT, z))
    for dy in range(4):
        for dx in range(4):
            if dx or dy:
                greet(dev((x + dx) % 4, 2 * ((y + dy) % 4) + c, z))

    for copy in locals_:
        copy.start()

    small[0].wait()
    ids = ids_ref[...]
    row = [ids[0:1, :], ids[1:2, :]]
    eye = iota((16, 16), 0) == iota((16, 16), 1)
    col = [jnp.sum(jnp.where(eye, r, 0), axis=1, keepdims=True) for r in row]
    low = iota((16, 16), 0) < iota((16, 16), 1)
    high = iota((16, 16), 1) < iota((16, 16), 0)

    def count(mask, axis):
        return jnp.sum(mask.astype(jnp.int32), axis=axis, keepdims=True)

    same00, same11 = col[0] == row[0], col[1] == row[1]
    slot_row = [
        count(same00 & low, 0),
        count(col[0] == row[1], 0) + count(same11 & low, 0),
    ]
    slot_col = [
        count(same00 & high, 1),
        count(col[1] == row[0], 1) + count(same11 & high, 1),
    ]

    place = iota((128, 16), 0)
    expert, m = place >> 4, place & 15
    chunk = chunk_of(m)
    slot = m - 5 * chunk
    taken = ((row[0] == expert) & (slot_row[0] == slot)) | ((row[1] == expert) & (slot_row[1] == slot))
    packed = jnp.zeros((128, 128), F32)
    small[1].wait()
    for k in range(3):
        mat = jnp.where(taken & (chunk == k), 1.0, 0.0).astype(BF)
        packed = packed + dot(mat, x_ref[:, k * 128 : (k + 1) * 128])
    pk[...] = packed.astype(BF).reshape(8, 16, 128)

    small[2].wait()
    logits = lax.dot_general(x_ref[...], rw_ref[...], (((1,), (1,)), ((), ())), preferred_element_type=F32)
    lp[...] = jnp.zeros((16, 128), F32)
    lp[:, 0:8] = logits

    pl.semaphore_wait(barrier, 15 + 7 + 15 + jnp.where(same, 0, 1))

    mine = 2 * zi + c
    for i in range(1, NZ):
        dz = (i + 1) // 2 if i % 2 else NZ - i // 2
        zt = (z + dz) % NZ
        start(pk.at[zt // 2], ra.at[mine], asend.at[0], arecv, dev(x, 2 * y + half, zt))

    @pl.when(same)
    def _():
        pltpu.make_async_copy(pk.at[zi], ra.at[mine], arecv).start()

    @pl.when(jnp.logical_not(same))
    def _():
        start(pk.at[zi], ra.at[mine], asend.at[1], arecv, dev(x, 2 * y + half, z))

    for dt in range(1, NT):
        start(lp, lr.at[dt - 1], lsend, lrecv, dev(x, (t + dt) % NT, z))

    sibling = dev(x, 2 * y + 1 - c, z)
    start(gate_hbm.at[0], wg.at[1], wsend.at[0], wrecv.at[0], sibling)
    start(up_hbm.at[0], wu.at[1], wsend.at[1], wrecv.at[1], sibling)
    start(down_hbm.at[0], wd.at[pl.ds(HID, HID)], wsend.at[2], wrecv.at[2], sibling)

    for copy in small[3:]:
        copy.wait()
    locals_[0].wait()
    locals_[1].wait()
    attention(q_ref, ck, cv, nk_ref, nv_ref, len_ref, att_ref)

    drain(ra, arecv)
    pick = iota((SLOTROWS, 256), 1)
    pm = pick & 15
    pc = chunk_of(pm)
    spot = ((pick >> 4) & 1) * 40 + (pick >> 5) * 5 + pm - 5 * pc
    here = spot == iota((SLOTROWS, 256), 0)
    arrived = ra[...].reshape(256, 128)
    for k in range(3):
        mat = jnp.where(here & (pc == k), 1.0, 0.0).astype(BF)
        ga[0, 0, :, k * 128 : (k + 1) * 128] = dot(mat, arrived).astype(BF)
    order = [(dx, dy) for dy in range(4) for dx in range(4) if dx or dy]
    for dx, dy in order:
        start(ga.at[0, 0], ga.at[dy, dx], gsend, grecv.at[dy], dev((x + dx) % 4, 2 * ((y + dy) % 4) + c, z))

    locals_[2].wait()
    locals_[3].wait()
    drain(wg.at[1], wrecv.at[0])
    drain(wu.at[1], wrecv.at[1])

    for dy in (0, 1, 3, 2):
        if dy == 0:
            drain(ga.at[0, pl.ds(1, 3)], grecv.at[0])
        else:
            drain(ga.at[dy], grecv.at[dy])
        for dx in range(4):
            for k in range(2):
                lhs[dx * 40 : (dx + 1) * 40, k * W : (k + 1) * W] = ga[dy, dx, k * 40 : (k + 1) * 40, :]
        rows = pl.ds(pl.multiple_of(((y + 4 - dy) % 4) * 768, 768), 768)
        a = lhs[...]
        for h in range(2):
            cols = slice(h * HID, (h + 1) * HID)
            g = dot(a, wg[h, rows, :])
            u = dot(a, wu[h, rows, :])
            if dy:
                g = g + accg[:, cols]
                u = u + accu[:, cols]
            if dy == 2:
                hid[:, cols] = (g / (1.0 + jnp.exp(-g)) * u).astype(BF)
            else:
                accg[:, cols] = g
                accu[:, cols] = u

    locals_[4].wait()
    drain(wd.at[pl.ds(HID, HID)], wrecv.at[2])
    for dy in (2, 1, 3, 0):
        yt = (y + dy) % 4
        term = dot(hid[...], wd[:, pl.ds(pl.multiple_of(yt * 768, 768), 768)]).astype(BF)
        for dx in range(4):
            block = (4 - dx) % 4
            to = rb if dx == 0 and dy == 0 else sb
            for k in range(2):
                to[dy, dx, k * 40 : (k + 1) * 40, :] = term[block * 40 : (block + 1) * 40, k * W : (k + 1) * W]
            if dx or dy:
                start(sb.at[dy, dx], rb.at[dy, dx], rsend, rrecv.at[dy], dev((x + dx) % 4, 2 * yt + c, z))

    total = rb[0, 0].astype(F32)
    for dy in (0, 1, 3, 2):
        if dy == 0:
            drain(rb.at[0, pl.ds(1, 3)], rrecv.at[0])
        else:
            drain(rb.at[dy], rrecv.at[dy])
        for dx in range(4):
            if dx or dy:
                total = total + rb[dy, dx].astype(F32)
    summed = total.astype(BF)

    place = iota((256, SLOTROWS), 0)
    m = place & 15
    chunk = chunk_of(m)
    spot = ((place >> 4) & 1) * 40 + (place >> 5) * 5 + m - 5 * chunk
    here = spot == iota((256, SLOTROWS), 1)
    back = jnp.zeros((256, 128), F32)
    for k in range(3):
        mat = jnp.where(here & (chunk == k), 1.0, 0.0).astype(BF)
        back = back + dot(mat, summed[:, k * 128 : (k + 1) * 128])
    pe[...] = back.astype(BF).reshape(16, 16, 128)
    for d in (4, 3, 5, 2, 6, 1, 7, 0):
        zt = (zi + d) % 8
        for b in range(2):
            ct = (c + b) % 2
            if d or b:
                start(pe.at[2 * zt + ct], rc.at[z], esend.at[0], erecv, dev(x, 2 * y + ct, 2 * zt + c))

    @pl.when(same)
    def _():
        pltpu.make_async_copy(pe.at[2 * zi + c], rc.at[z], erecv).start()

    @pl.when(jnp.logical_not(same))
    def _():
        start(pe.at[2 * zi + c], rc.at[z], esend.at[1], erecv, dev(x, t, 2 * zi + c))

    drain(lr, lrecv)
    full = lp[...]
    for dt in range(NT - 1):
        full = full + lr[dt]
    lane = iota((16, 128), 1)
    chosen = [jnp.sum(jnp.where(lane == col[k], full, 0.0), axis=1, keepdims=True) for k in range(2)]
    mixing = [1.0 / (1.0 + jnp.exp(chosen[1 - k] - chosen[k])) for k in range(2)]

    place = iota((16, 256), 1)
    m = place & 15
    chunk = chunk_of(m)
    slot = m - 5 * chunk
    own = [(col[k] == (place >> 5)) & (slot_col[k] == slot) for k in range(2)]
    drain(rc, erecv)
    returned = rc[...].reshape(256, 128)
    for k in range(3):
        value = [
            dot(jnp.where(own[j] & (chunk == k), 1.0, 0.0).astype(BF), returned) for j in range(2)
        ]
        out_ref[:, k * 128 : (k + 1) * 128] = (mixing[0] * value[0] + mixing[1] * value[1]).astype(BF)

    drain(ra.at[pl.ds(0, 15)], asend.at[0])
    drain(rc.at[pl.ds(0, 15)], esend.at[0])

    @pl.when(jnp.logical_not(same))
    def _():
        drain(ra.at[0], asend.at[1])
        drain(rc.at[0], esend.at[1])

    drain(lr, lsend)
    drain(wg.at[1], wsend.at[0])
    drain(wu.at[1], wsend.at[1])
    drain(wd.at[pl.ds(HID, HID)], wsend.at[2])
    for dy in range(4):
        if dy == 0:
            drain(ga.at[0, pl.ds(1, 3)], gsend)
            drain(rb.at[0, pl.ds(1, 3)], rsend)
        else:
            drain(ga.at[dy], gsend)
            drain(rb.at[dy], rsend)


def body(
    queries, cache_keys, cache_values, new_keys, new_values, lengths,
    moe_input, router_weight, expert_ids, gate_weight, up_weight, down_weight,
):
    vm = pl.BlockSpec(memory_space=pltpu.VMEM)
    hbm = pl.BlockSpec(memory_space=pltpu.HBM)
    dma = pltpu.SemaphoreType.DMA
    return pl.pallas_call(
        kernel,
        out_shape=(
            jax.ShapeDtypeStruct((1, 768), BF),
            jax.ShapeDtypeStruct((16, W), BF),
        ),
        in_specs=[hbm] * 12,
        out_specs=(vm, vm),
        scratch_shapes=[
            pltpu.VMEM((1, 768), BF),
            pltpu.VMEM((1, 128), BF),
            pltpu.VMEM((1, 128), BF),
            pltpu.VMEM((1, 1), jnp.int32),
            pltpu.VMEM((16, W), BF),
            pltpu.VMEM((8, W), BF),
            pltpu.VMEM((2, 16), jnp.int32),
            pltpu.VMEM((512, 128), BF),
            pltpu.VMEM((512, 128), BF),
            pltpu.VMEM((2, D, HID), BF),
            pltpu.VMEM((2, D, HID), BF),
            pltpu.VMEM((2 * HID, D), BF),
            pltpu.VMEM((8, 16, 128), BF),
            pltpu.VMEM((16, 16, 128), BF),
            pltpu.VMEM((4, 4, SLOTROWS, W), BF),
            pltpu.VMEM((160, 768), BF),
            pltpu.VMEM((160, 2 * HID), F32),
            pltpu.VMEM((160, 2 * HID), F32),
            pltpu.VMEM((160, 2 * HID), BF),
            pltpu.VMEM((4, 4, SLOTROWS, W), BF),
            pltpu.VMEM((4, 4, SLOTROWS, W), BF),
            pltpu.VMEM((16, 16, 128), BF),
            pltpu.VMEM((16, 16, 128), BF),
            pltpu.VMEM((16, 128), F32),
            pltpu.VMEM((7, 16, 128), F32),
            dma((7,)),
            dma((5,)),
            dma((3,)),
            dma((3,)),
            dma((2,)),
            dma,
            dma,
            dma((4,)),
            dma,
            dma((4,)),
            dma((2,)),
            dma,
            dma,
            dma,
        ],
        compiler_params=pltpu.CompilerParams(
            collective_id=0, has_side_effects=True, vmem_limit_bytes=60 * 1024 * 1024
        ),
        cost_estimate=pl.CostEstimate(flops=1600000000, bytes_accessed=5500000, transcendentals=100000),
    )(
        queries, cache_keys, cache_values, new_keys, new_values, lengths.reshape(1, 1),
        moe_input, router_weight, expert_ids.T, gate_weight, up_weight, down_weight,
    )


def solution(mesh):
    placed = (
        P(("attn", "exp"), "tp"),
        P(("attn", "exp"), None, "tp"),
        P(("attn", "exp"), None, "tp"),
        P(("attn", "exp"), "tp"),
        P(("attn", "exp"), "tp"),
        P(("attn", "exp")),
        P(("attn", "exp"), "tp"),
        P(None, "tp"),
        P(("attn", "exp"), None),
        P("exp", None, ("attn", "tp")),
        P("exp", None, ("attn", "tp")),
        P("exp", ("attn", "tp"), None),
    )
    return jax.shard_map(
        body,
        mesh=mesh,
        in_specs=placed,
        out_specs=(P(("attn", "exp"), "tp"), P(("attn", "exp"), "tp")),
        check_vma=False,
    )
```

```python
import math

import jax
import jax.numpy as jnp
from jax import lax
from jax.experimental import pallas as pl
from jax.experimental.pallas import tpu as pltpu
from jax.sharding import PartitionSpec as P

MESH = pl.DeviceIdType.MESH
BF = jnp.bfloat16
F32 = jnp.float32
NT = 8
W = 384
NG = 4
GS = 8 // NG
RAW = 32 * GS
NEAR = (0, 1, -1, 2, -2, 3, -3, 4)
PLANE = tuple((dx, dy) for dy in (2, 1, 3, 0) for dx in (2, 1, 3, 0) if dx or dy)
HID = 256
D = 3072


def iota(shape, dim):
    return lax.broadcasted_iota(jnp.int32, shape, dim)


def chunk_of(m):
    return (m >= 5).astype(jnp.int32) + (m >= 10).astype(jnp.int32) + (m >= 15).astype(jnp.int32)


def dot(a, b):
    return jnp.dot(a, b, preferred_element_type=F32)


def drain(ref, sem):
    pltpu.make_async_copy(ref, ref, sem).wait()


def attention(q_ref, ck, cv, nk_ref, nv_ref, len_ref, att_ref):
    scale = 1.0 / math.sqrt(128)
    q = q_ref[...]
    heads = [q[:, h * 128 : (h + 1) * 128] for h in range(6)]
    qh = jnp.concatenate(heads + [jnp.zeros((2, 128), BF)], axis=0)
    scores = lax.dot_general(qh, ck[...], (((1,), (1,)), ((), ())), preferred_element_type=F32) * scale
    own = jnp.sum(qh.astype(F32) * nk_ref[...].astype(F32), axis=1, keepdims=True) * scale
    visible = iota(scores.shape, 1) < len_ref[...]
    scores = jnp.where(visible, scores, -jnp.inf)
    peak = jnp.maximum(jnp.max(scores, axis=1, keepdims=True), own)
    weights = jnp.exp(scores - peak)
    own_weight = jnp.exp(own - peak)
    total = jnp.sum(weights, axis=1, keepdims=True) + own_weight
    probs = (weights / total).astype(BF)
    own_prob = (own_weight / total).astype(BF).astype(F32)
    result = dot(probs, cv[...]) + own_prob * nv_ref[...].astype(F32)
    result = result.astype(BF)
    for h in range(6):
        att_ref[:, h * 128 : (h + 1) * 128] = result[h : h + 1, :]


def kernel(
    q_hbm, ck_hbm, cv_hbm, nk_hbm, nv_hbm, len_hbm, x_hbm, rw_hbm, ids_hbm, gate_hbm, up_hbm, down_hbm,
    att_ref, out_ref,
    q_ref, nk_ref, nv_ref, len_ref, x_ref, rw_ref, ids_ref, ck, cv, wg, wu, wd,
    pk, ga, lhs, hid, sb, rb, pe, rc, lp, lr,
    small_sem, loc_sem, wsend, wrecv, asend, arecv, gsend, grecv, rsend, rrecv, esend, erecv, lsend, lrecv,
):
    x = lax.axis_index("attn")
    t = lax.axis_index("tp")
    z = lax.axis_index("exp")
    y = t // 2
    c = t % 2
    half = z % 2
    zi = z // 2
    same = half == c

    def start(src, dst, ssem, rsem, device):
        pltpu.make_async_remote_copy(
            src_ref=src, dst_ref=dst, send_sem=ssem, recv_sem=rsem, device_id=device, device_id_type=MESH
        ).start()

    barrier = pltpu.get_barrier_semaphore()

    def greet(device):
        pl.semaphore_signal(barrier, inc=1, device_id=device, device_id_type=MESH)

    turn = jnp.where((c == 1) & (half == 0), -1, 1)
    source = [2 * ((zi + turn * NEAR[p] + 8) % 8) + c for p in range(8)]

    for p in reversed(range(8)):
        greet((x, 2 * y + 1 - c, source[p]))
        if p:
            greet((x, t, source[p]))

    @pl.when(jnp.logical_not(same))
    def _():
        greet((x, t, source[0]))

    for dx, dy in PLANE:
        greet(((x + dx) % 4, 2 * ((y + dy) % 4) + c, z))
    for dt in range(1, NT):
        greet((x, (t + dt) % NT, z))

    small = [
        pltpu.make_async_copy(src, dst, small_sem.at[i])
        for i, (src, dst) in enumerate([
            (ids_hbm, ids_ref), (x_hbm, x_ref), (rw_hbm, rw_ref), (q_hbm, q_ref),
            (nk_hbm, nk_ref), (nv_hbm, nv_ref), (len_hbm, len_ref),
        ])
    ]
    large = [
        pltpu.make_async_copy(ck_hbm.at[0], ck, loc_sem.at[0]),
        pltpu.make_async_copy(cv_hbm.at[0], cv, loc_sem.at[1]),
        pltpu.make_async_copy(gate_hbm.at[0], wg.at[0], loc_sem.at[2]),
        pltpu.make_async_copy(up_hbm.at[0], wu.at[0], loc_sem.at[3]),
        pltpu.make_async_copy(down_hbm.at[0], wd.at[pl.ds(0, HID)], loc_sem.at[4]),
    ]
    for copy in small:
        copy.start()
    for copy in large:
        copy.start()

    small[0].wait()
    ids = ids_ref[...]
    row = [ids[0:1, :], ids[1:2, :]]
    eye = iota((16, 16), 0) == iota((16, 16), 1)
    col = [jnp.sum(jnp.where(eye, r, 0), axis=1, keepdims=True) for r in row]
    low = iota((16, 16), 0) < iota((16, 16), 1)
    high = iota((16, 16), 1) < iota((16, 16), 0)

    def count(mask, axis):
        return jnp.sum(mask.astype(jnp.int32), axis=axis, keepdims=True)

    same00, same11 = col[0] == row[0], col[1] == row[1]
    slot_row = [
        count(same00 & low, 0),
        count(col[0] == row[1], 0) + count(same11 & low, 0),
    ]
    slot_col = [
        count(same00 & high, 1),
        count(col[1] == row[0], 1) + count(same11 & high, 1),
    ]

    place = iota((128, 16), 0)
    expert, m = place >> 4, place & 15
    chunk = chunk_of(m)
    slot = m - 5 * chunk
    taken = ((row[0] == expert) & (slot_row[0] == slot)) | ((row[1] == expert) & (slot_row[1] == slot))
    packed = jnp.zeros((128, 128), F32)
    small[1].wait()
    for k in range(3):
        mat = jnp.where(taken & (chunk == k), 1.0, 0.0).astype(BF)
        packed = packed + dot(mat, x_ref[:, k * 128 : (k + 1) * 128])
    pk[...] = packed.astype(BF).reshape(8, 16, 128)

    small[2].wait()
    logits = lax.dot_general(x_ref[...], rw_ref[...], (((1,), (1,)), ((), ())), preferred_element_type=F32)
    lp[...] = jnp.zeros((16, 128), F32)
    lp[:, 0:8] = logits

    pl.semaphore_wait(barrier, 15 + 7 + 15 + jnp.where(same, 0, 1))

    def spot(p):
        return ga.at[p // GS, 0, pl.ds(pl.multiple_of(16 * (2 * (p % GS) + c), 16), 16)]

    for p in reversed(range(8)):
        for b in range(2):
            sign = jnp.where((half == 1) & (b == 0), -1, 1)
            target = (zi - sign * NEAR[p] + 8) % 8
            if p:
                start(pk.at[target], spot(p), asend.at[0], arecv.at[p // GS], (x, 2 * y + half, 2 * target + b))
            else:
                @pl.when(half != b)
                def _(target=target, b=b):
                    start(pk.at[target], spot(0), asend.at[0], arecv.at[0], (x, 2 * y + half, 2 * target + b))

    @pl.when(same)
    def _():
        pltpu.make_async_copy(pk.at[zi], spot(0), arecv.at[0]).start()

    @pl.when(jnp.logical_not(same))
    def _():
        start(pk.at[zi], spot(0), asend.at[1], arecv.at[0], (x, 2 * y + half, z))

    sibling = (x, 2 * y + 1 - c, z)
    start(gate_hbm.at[0], wg.at[1], wsend.at[0], wrecv.at[0], sibling)
    start(up_hbm.at[0], wu.at[1], wsend.at[1], wrecv.at[1], sibling)
    start(down_hbm.at[0], wd.at[pl.ds(HID, HID)], wsend.at[2], wrecv.at[2], sibling)

    for dt in range(1, NT):
        start(lp, lr.at[dt - 1], lsend, lrecv, (x, (t + dt) % NT, z))

    for copy in small[3:]:
        copy.wait()
    large[0].wait()
    large[1].wait()
    attention(q_ref, ck, cv, nk_ref, nv_ref, len_ref, att_ref)

    for g in range(NG):
        drain(ga.at[g, 0], arecv.at[g])
        for dx, dy in PLANE:
            start(
                ga.at[g, 0], ga.at[g, 4 * dy + dx], gsend, grecv.at[g],
                ((x + dx) % 4, 2 * ((y + dy) % 4) + c, z),
            )

    for copy in large[2:]:
        copy.wait()
    drain(wg.at[1], wrecv.at[0])
    drain(wu.at[1], wrecv.at[1])
    drain(wd.at[pl.ds(HID, HID)], wrecv.at[2])

    def piece_row(raw):
        m = raw & 15
        chunk = chunk_of(m)
        inner = (raw >> 5) * 5 + m - 5 * chunk
        return jnp.where(chunk == 3, -1, (((raw >> 4) & 1) * 3 + chunk) * 16 + inner)

    unpack = jnp.where(piece_row(iota((96, RAW), 1)) == iota((96, RAW), 0), 1.0, 0.0).astype(BF)
    repack = jnp.where(piece_row(iota((RAW, 96), 0)) == iota((RAW, 96), 1), 1.0, 0.0).astype(BF)

    def group(g, _):
        drain(ga.at[g, pl.ds(1, 15)], grecv.at[g])
        for dy in range(4):
            raw = jnp.concatenate([ga[g, 4 * dy + dx] for dx in range(4)], axis=1)
            rows = dot(unpack, raw).astype(BF)
            for dx in range(4):
                for k in range(6):
                    lhs[dx * 16 : (dx + 1) * 16, dy * 768 + k * 128 : dy * 768 + (k + 1) * 128] = rows[
                        k * 16 : (k + 1) * 16, dx * 128 : (dx + 1) * 128
                    ]
        for h in range(2):
            gate = jnp.zeros((64, HID), F32)
            up = jnp.zeros((64, HID), F32)
            for dy in range(4):
                a = lhs[:, dy * 768 : (dy + 1) * 768]
                features = pl.ds(pl.multiple_of(((y + 4 - dy) % 4) * 768, 768), 768)
                gate = gate + dot(a, wg[h, features, :])
                up = up + dot(a, wu[h, features, :])
            hid[:, h * HID : (h + 1) * HID] = (gate / (1.0 + jnp.exp(-gate)) * up).astype(BF)
        for dy in (2, 1, 3, 0):
            yt = (y + dy) % 4
            term = dot(hid[...], wd[:, pl.ds(pl.multiple_of(yt * 768, 768), 768)]).astype(BF)
            blocks = [(4 - dx) % 4 for dx in range(4)]
            stacked = jnp.concatenate(
                [
                    jnp.concatenate([term[b * 16 : (b + 1) * 16, k * 128 : (k + 1) * 128] for b in blocks], axis=1)
                    for k in range(6)
                ],
                axis=0,
            )
            back = dot(repack, stacked).astype(BF)
            for dx in range(4):
                sb[g, 4 * dy + dx] = back[:, dx * 128 : (dx + 1) * 128]
            for dx in (2, 1, 3, 0):
                if dx or dy:
                    start(
                        sb.at[g, 4 * dy + dx], rb.at[g, 4 * dy + dx], rsend, rrecv.at[g],
                        ((x + dx) % 4, 2 * yt + c, z),
                    )
        return 0

    lax.fori_loop(0, NG, group, 0)

    for g in range(NG):
        drain(rb.at[g, pl.ds(1, 15)], rrecv.at[g])
        total = sb[g, 0].astype(F32)
        for i in range(1, 16):
            total = total + rb[g, i].astype(F32)
        pe[g] = total.astype(BF)
        for q in range(GS):
            p = g * GS + q
            for b in range(2):
                ct = (c + b) % 2
                message = pe.at[g, pl.ds(pl.multiple_of(16 * (2 * q + ct), 16), 16)]
                if p or b:
                    start(message, rc.at[z], esend.at[0], erecv, (x, 2 * y + ct, source[p]))
                else:
                    @pl.when(same)
                    def _(message=message):
                        pltpu.make_async_copy(message, rc.at[z], erecv).start()

                    @pl.when(jnp.logical_not(same))
                    def _(message=message):
                        start(message, rc.at[z], esend.at[1], erecv, (x, t, source[0]))

    drain(lr, lrecv)
    full = lp[...]
    for dt in range(NT - 1):
        full = full + lr[dt]
    lane = iota((16, 128), 1)
    chosen = [jnp.sum(jnp.where(lane == col[k], full, 0.0), axis=1, keepdims=True) for k in range(2)]
    mixing = [1.0 / (1.0 + jnp.exp(chosen[1 - k] - chosen[k])) for k in range(2)]

    place = iota((16, 256), 1)
    m = place & 15
    chunk = chunk_of(m)
    slot = m - 5 * chunk
    own = [(col[k] == (place >> 5)) & (slot_col[k] == slot) for k in range(2)]
    picks = [[jnp.where(own[j] & (chunk == k), 1.0, 0.0).astype(BF) for j in range(2)] for k in range(3)]
    drain(rc, erecv)
    returned = rc[...].reshape(256, 128)
    for k in range(3):
        value = [dot(picks[k][j], returned) for j in range(2)]
        out_ref[:, k * 128 : (k + 1) * 128] = (mixing[0] * value[0] + mixing[1] * value[1]).astype(BF)

    drain(rc.at[pl.ds(0, 15)], asend.at[0])
    drain(rc.at[pl.ds(0, 15)], esend.at[0])

    @pl.when(jnp.logical_not(same))
    def _():
        drain(rc.at[0], asend.at[1])
        drain(rc.at[0], esend.at[1])

    drain(lr, lsend)
    drain(wg.at[1], wsend.at[0])
    drain(wu.at[1], wsend.at[1])
    drain(wd.at[pl.ds(HID, HID)], wsend.at[2])
    drain(ga.at[:, pl.ds(1, 15)], gsend)
    drain(rb.at[:, pl.ds(1, 15)], rsend)


def body(
    queries, cache_keys, cache_values, new_keys, new_values, lengths,
    moe_input, router_weight, expert_ids, gate_weight, up_weight, down_weight,
):
    vm = pl.BlockSpec(memory_space=pltpu.VMEM)
    hbm = pl.BlockSpec(memory_space=pltpu.HBM)
    dma = pltpu.SemaphoreType.DMA
    return pl.pallas_call(
        kernel,
        out_shape=(
            jax.ShapeDtypeStruct((1, 768), BF),
            jax.ShapeDtypeStruct((16, W), BF),
        ),
        in_specs=[hbm] * 12,
        out_specs=(vm, vm),
        scratch_shapes=[
            pltpu.VMEM((1, 768), BF),
            pltpu.VMEM((1, 128), BF),
            pltpu.VMEM((1, 128), BF),
            pltpu.VMEM((1, 1), jnp.int32),
            pltpu.VMEM((16, W), BF),
            pltpu.VMEM((8, W), BF),
            pltpu.VMEM((2, 16), jnp.int32),
            pltpu.VMEM((512, 128), BF),
            pltpu.VMEM((512, 128), BF),
            pltpu.VMEM((2, D, HID), BF),
            pltpu.VMEM((2, D, HID), BF),
            pltpu.VMEM((2 * HID, D), BF),
            pltpu.VMEM((8, 16, 128), BF),
            pltpu.VMEM((NG, 16, RAW, 128), BF),
            pltpu.VMEM((64, D), BF),
            pltpu.VMEM((64, 2 * HID), BF),
            pltpu.VMEM((NG, 16, RAW, 128), BF),
            pltpu.VMEM((NG, 16, RAW, 128), BF),
            pltpu.VMEM((NG, RAW, 128), BF),
            pltpu.VMEM((16, 16, 128), BF),
            pltpu.VMEM((16, 128), F32),
            pltpu.VMEM((7, 16, 128), F32),
            dma((7,)),
            dma((5,)),
            dma((3,)),
            dma((3,)),
            dma((2,)),
            dma((NG,)),
            dma,
            dma((NG,)),
            dma,
            dma((NG,)),
            dma((2,)),
            dma,
            dma,
            dma,
        ],
        compiler_params=pltpu.CompilerParams(
            collective_id=0, has_side_effects=True, vmem_limit_bytes=60 * 1024 * 1024
        ),
        cost_estimate=pl.CostEstimate(flops=1600000000, bytes_accessed=5500000, transcendentals=100000),
    )(
        queries, cache_keys, cache_values, new_keys, new_values, lengths.reshape(1, 1),
        moe_input, router_weight, expert_ids.T, gate_weight, up_weight, down_weight,
    )


def solution(mesh):
    placed = (
        P(("attn", "exp"), "tp"),
        P(("attn", "exp"), None, "tp"),
        P(("attn", "exp"), None, "tp"),
        P(("attn", "exp"), "tp"),
        P(("attn", "exp"), "tp"),
        P(("attn", "exp")),
        P(("attn", "exp"), "tp"),
        P(None, "tp"),
        P(("attn", "exp"), None),
        P("exp", None, ("attn", "tp")),
        P("exp", None, ("attn", "tp")),
        P("exp", ("attn", "tp"), None),
    )
    return jax.shard_map(
        body,
        mesh=mesh,
        in_specs=placed,
        out_specs=(P(("attn", "exp"), "tp"), P(("attn", "exp"), "tp")),
        check_vma=False,
    )
```

```python
import math

import jax
import jax.numpy as jnp
from jax import lax
from jax.experimental import pallas as pl
from jax.experimental.pallas import tpu as pltpu
from jax.sharding import PartitionSpec as P

MESH = pl.DeviceIdType.MESH
BF = jnp.bfloat16
F32 = jnp.float32
NT = 8
W = 384
NG = 4
GS = 8 // NG
RAW = 32 * GS
BLK = 8 * GS
STEPS = ((2, 1, 3, 0),)
SPREAD = (0, 1, 3, 2)
WORK = (0, 1, 3, 2)
LATE = (0,)
BACK = (1, 3, 2, 0)
NEAR = (0, 1, -1, 2, -2, 3, -3, 4)
PLANE = tuple((dx, dy) for dy in (2, 1, 3, 0) for dx in (2, 1, 3, 0) if dx or dy)
HID = 256
D = 3072


def iota(shape, dim):
    return lax.broadcasted_iota(jnp.int32, shape, dim)


def chunk_of(m):
    return (m >= 5).astype(jnp.int32) + (m >= 10).astype(jnp.int32) + (m >= 15).astype(jnp.int32)


def dot(a, b):
    return jnp.dot(a, b, preferred_element_type=F32)


def drain(ref, sem):
    pltpu.make_async_copy(ref, ref, sem).wait()


def attention(q_ref, ck, cv, nk_ref, nv_ref, len_ref, att_ref):
    scale = 1.0 / math.sqrt(128)
    q = q_ref[...]
    heads = [q[:, h * 128 : (h + 1) * 128] for h in range(6)]
    qh = jnp.concatenate(heads + [jnp.zeros((2, 128), BF)], axis=0)
    scores = lax.dot_general(qh, ck[...], (((1,), (1,)), ((), ())), preferred_element_type=F32) * scale
    own = jnp.sum(qh.astype(F32) * nk_ref[...].astype(F32), axis=1, keepdims=True) * scale
    visible = iota(scores.shape, 1) < len_ref[...]
    scores = jnp.where(visible, scores, -jnp.inf)
    peak = jnp.maximum(jnp.max(scores, axis=1, keepdims=True), own)
    weights = jnp.exp(scores - peak)
    own_weight = jnp.exp(own - peak)
    total = jnp.sum(weights, axis=1, keepdims=True) + own_weight
    probs = (weights / total).astype(BF)
    own_prob = (own_weight / total).astype(BF).astype(F32)
    result = dot(probs, cv[...]) + own_prob * nv_ref[...].astype(F32)
    result = result.astype(BF)
    for h in range(6):
        att_ref[:, h * 128 : (h + 1) * 128] = result[h : h + 1, :]


def kernel(
    q_hbm, ck_hbm, cv_hbm, nk_hbm, nv_hbm, len_hbm, x_hbm, rw_hbm, ids_hbm, gate_hbm, up_hbm, down_hbm,
    att_ref, out_ref,
    q_ref, nk_ref, nv_ref, len_ref, x_ref, rw_ref, ids_ref, ck, cv, wg, wu, wd,
    pk, ga, lhs, hid, sb, rb, pe, rc, lp, lr,
    small_sem, loc_sem, wsend, wrecv, asend, arecv, gsend, grecv, rsend, rrecv, esend, erecv, lsend, lrecv,
):
    x = lax.axis_index("attn")
    t = lax.axis_index("tp")
    z = lax.axis_index("exp")
    y = t // 2
    c = t % 2
    odd = z % 2
    half = 1 - odd
    zi = z // 2
    same = half == c

    def start(src, dst, ssem, rsem, device):
        pltpu.make_async_remote_copy(
            src_ref=src, dst_ref=dst, send_sem=ssem, recv_sem=rsem, device_id=device, device_id_type=MESH
        ).start()

    barrier = pltpu.get_barrier_semaphore()

    def greet(device):
        pl.semaphore_signal(barrier, inc=1, device_id=device, device_id_type=MESH)

    turn = jnp.where((c == 0) & (odd == 0), -1, 1)
    source = [2 * ((zi + turn * NEAR[p] + 8) % 8) + 1 - c for p in range(8)]

    for p in reversed(range(8)):
        greet((x, 2 * y + 1 - c, source[p]))
        if p:
            greet((x, t, source[p]))

    @pl.when(jnp.logical_not(same))
    def _():
        greet((x, t, source[0]))

    for dx, dy in PLANE:
        greet(((x + dx) % 4, 2 * ((y + dy) % 4) + c, z))
    for dt in range(1, NT):
        greet((x, (t + dt) % NT, z))

    small = [
        pltpu.make_async_copy(src, dst, small_sem.at[i])
        for i, (src, dst) in enumerate([
            (ids_hbm, ids_ref), (x_hbm, x_ref), (rw_hbm, rw_ref), (q_hbm, q_ref),
            (nk_hbm, nk_ref), (nv_hbm, nv_ref), (len_hbm, len_ref),
        ])
    ]
    large = [
        pltpu.make_async_copy(ck_hbm.at[0], ck, loc_sem.at[0]),
        pltpu.make_async_copy(cv_hbm.at[0], cv, loc_sem.at[1]),
        pltpu.make_async_copy(gate_hbm.at[0], wg.at[0], loc_sem.at[2]),
        pltpu.make_async_copy(up_hbm.at[0], wu.at[0], loc_sem.at[3]),
        pltpu.make_async_copy(down_hbm.at[0], wd.at[pl.ds(0, HID)], loc_sem.at[4]),
    ]
    for copy in small:
        copy.start()
    for copy in large:
        copy.start()

    small[0].wait()
    ids = ids_ref[...]
    row = [ids[0:1, :], ids[1:2, :]]
    eye = iota((16, 16), 0) == iota((16, 16), 1)
    col = [jnp.sum(jnp.where(eye, r, 0), axis=1, keepdims=True) for r in row]
    low = iota((16, 16), 0) < iota((16, 16), 1)
    high = iota((16, 16), 1) < iota((16, 16), 0)

    def count(mask, axis):
        return jnp.sum(mask.astype(jnp.int32), axis=axis, keepdims=True)

    same00, same11 = col[0] == row[0], col[1] == row[1]
    slot_row = [
        count(same00 & low, 0),
        count(col[0] == row[1], 0) + count(same11 & low, 0),
    ]
    slot_col = [
        count(same00 & high, 1),
        count(col[1] == row[0], 1) + count(same11 & high, 1),
    ]

    place = iota((128, 16), 0)
    expert, m = place >> 4, place & 15
    chunk = chunk_of(m)
    slot = m - 5 * chunk
    taken = ((row[0] == expert) & (slot_row[0] == slot)) | ((row[1] == expert) & (slot_row[1] == slot))
    packed = jnp.zeros((128, 128), F32)
    small[1].wait()
    for k in range(3):
        mat = jnp.where(taken & (chunk == k), 1.0, 0.0).astype(BF)
        packed = packed + dot(mat, x_ref[:, k * 128 : (k + 1) * 128])
    pk[...] = packed.astype(BF).reshape(8, 16, 128)

    small[2].wait()
    logits = lax.dot_general(x_ref[...], rw_ref[...], (((1,), (1,)), ((), ())), preferred_element_type=F32)
    lp[...] = jnp.zeros((16, 128), F32)
    lp[:, 0:8] = logits

    pl.semaphore_wait(barrier, 15 + 7 + 15 + jnp.where(same, 0, 1))

    def spot(p):
        return ga.at[p // GS, 0, pl.ds(pl.multiple_of(16 * (2 * (p % GS) + c), 16), 16)]

    for p in reversed(range(8)):
        for b in range(2):
            sign = jnp.where((odd == 1) & (b == 0), -1, 1)
            target = (zi - sign * NEAR[p] + 8) % 8
            if p:
                start(pk.at[target], spot(p), asend.at[0], arecv.at[p // GS], (x, 2 * y + half, 2 * target + b))
            else:
                @pl.when(odd != b)
                def _(target=target, b=b):
                    start(pk.at[target], spot(0), asend.at[0], arecv.at[0], (x, 2 * y + half, 2 * target + b))

    @pl.when(same)
    def _():
        pltpu.make_async_copy(pk.at[zi], spot(0), arecv.at[0]).start()

    @pl.when(jnp.logical_not(same))
    def _():
        start(pk.at[zi], spot(0), asend.at[1], arecv.at[0], (x, 2 * y + half, z))

    sibling = (x, 2 * y + 1 - c, z)
    start(gate_hbm.at[0], wg.at[1], wsend.at[0], wrecv.at[0], sibling)
    start(up_hbm.at[0], wu.at[1], wsend.at[1], wrecv.at[1], sibling)
    start(down_hbm.at[0], wd.at[pl.ds(HID, HID)], wsend.at[2], wrecv.at[2], sibling)

    for dt in range(1, NT):
        start(lp, lr.at[dt - 1], lsend, lrecv, (x, (t + dt) % NT, z))

    for copy in small[3:]:
        copy.wait()
    large[0].wait()
    large[1].wait()
    attention(q_ref, ck, cv, nk_ref, nv_ref, len_ref, att_ref)

    for g in SPREAD:
        drain(ga.at[g, 0], arecv.at[g])
        for dx, dy in PLANE:
            start(
                ga.at[g, 0], ga.at[g, 4 * dy + dx], gsend, grecv.at[g],
                ((x + dx) % 4, 2 * ((y + dy) % 4) + c, z),
            )

    for copy in large[2:]:
        copy.wait()
    drain(wg.at[1], wrecv.at[0])
    drain(wu.at[1], wrecv.at[1])
    drain(wd.at[pl.ds(HID, HID)], wrecv.at[2])

    def piece_row(raw):
        m = raw & 15
        chunk = chunk_of(m)
        inner = (raw >> 5) * 5 + m - 5 * chunk
        return jnp.where(chunk == 3, -1, (((raw >> 4) & 1) * 3 + chunk) * BLK + inner)

    pieces = 6 * BLK
    unpack = jnp.where(piece_row(iota((pieces, RAW), 1)) == iota((pieces, RAW), 0), 1.0, 0.0).astype(BF)
    repack = jnp.where(piece_row(iota((RAW, pieces), 0)) == iota((RAW, pieces), 1), 1.0, 0.0).astype(BF)

    def compute(g, send):
        for dy in range(4):
            raw = jnp.concatenate([ga[g, 4 * dy + dx] for dx in range(4)], axis=1)
            rows = dot(unpack, raw).astype(BF)
            for dx in range(4):
                for k in range(6):
                    lhs[dx * BLK : (dx + 1) * BLK, dy * 768 + k * 128 : dy * 768 + (k + 1) * 128] = rows[
                        k * BLK : (k + 1) * BLK, dx * 128 : (dx + 1) * 128
                    ]
        for h in range(2):
            gate = jnp.zeros((4 * BLK, HID), F32)
            up = jnp.zeros((4 * BLK, HID), F32)
            for dy in range(4):
                a = lhs[:, dy * 768 : (dy + 1) * 768]
                features = pl.ds(pl.multiple_of(((y + 4 - dy) % 4) * 768, 768), 768)
                gate = gate + dot(a, wg[h, features, :])
                up = up + dot(a, wu[h, features, :])
            hid[:, h * HID : (h + 1) * HID] = (gate / (1.0 + jnp.exp(-gate)) * up).astype(BF)
        blocks = [(4 - dx) % 4 for dx in range(4)]
        for step in STEPS:
            terms = []
            for dy in step:
                features = pl.ds(pl.multiple_of(((y + dy) % 4) * 768, 768), 768)
                terms.append(dot(hid[...], wd[:, features]).astype(BF))
            for dy, term in zip(step, terms):
                stacked = jnp.concatenate(
                    [
                        jnp.concatenate([term[b * BLK : (b + 1) * BLK, k * 128 : (k + 1) * 128] for b in blocks], axis=1)
                        for k in range(6)
                    ],
                    axis=0,
                )
                back = dot(repack, stacked).astype(BF)
                for dx in range(4):
                    sb[g, 4 * dy + dx] = back[:, dx * 128 : (dx + 1) * 128]
            if send:
                for dy in step:
                    send_sums(g, dy)

    def send_sums(g, dy):
        for dx in (2, 1, 3, 0):
            if dx or dy:
                start(
                    sb.at[g, 4 * dy + dx], rb.at[g, 4 * dy + dx], rsend, rrecv.at[g],
                    ((x + dx) % 4, 2 * ((y + dy) % 4) + c, z),
                )

    for g in WORK:
        drain(ga.at[g, pl.ds(1, 15)], grecv.at[g])
        compute(g, g not in LATE)
    for g in LATE:
        for dy in (2, 1, 3, 0):
            send_sums(g, dy)

    for g in BACK:
        drain(rb.at[g, pl.ds(1, 15)], rrecv.at[g])
        total = sb[g, 0].astype(F32)
        for i in range(1, 16):
            total = total + rb[g, i].astype(F32)
        pe[g] = total.astype(BF)
        for q in range(GS):
            p = g * GS + q
            for b in range(2):
                ct = (c + b) % 2
                message = pe.at[g, pl.ds(pl.multiple_of(16 * (2 * q + ct), 16), 16)]
                if p or b:
                    start(message, rc.at[z], esend.at[0], erecv, (x, 2 * y + ct, source[p]))
                else:
                    @pl.when(same)
                    def _(message=message):
                        pltpu.make_async_copy(message, rc.at[z], erecv).start()

                    @pl.when(jnp.logical_not(same))
                    def _(message=message):
                        start(message, rc.at[z], esend.at[1], erecv, (x, t, source[0]))

    drain(lr, lrecv)
    full = lp[...]
    for dt in range(NT - 1):
        full = full + lr[dt]
    lane = iota((16, 128), 1)
    chosen = [jnp.sum(jnp.where(lane == col[k], full, 0.0), axis=1, keepdims=True) for k in range(2)]
    mixing = [1.0 / (1.0 + jnp.exp(chosen[1 - k] - chosen[k])) for k in range(2)]

    place = iota((16, 256), 1)
    m = place & 15
    chunk = chunk_of(m)
    slot = m - 5 * chunk
    own = [(col[k] == (place >> 5)) & (slot_col[k] == slot) for k in range(2)]
    picks = [[jnp.where(own[j] & (chunk == k), 1.0, 0.0).astype(BF) for j in range(2)] for k in range(3)]
    drain(rc, erecv)
    returned = rc[...].reshape(256, 128)
    for k in range(3):
        value = [dot(picks[k][j], returned) for j in range(2)]
        out_ref[:, k * 128 : (k + 1) * 128] = (mixing[0] * value[0] + mixing[1] * value[1]).astype(BF)

    drain(rc.at[pl.ds(0, 15)], asend.at[0])
    drain(rc.at[pl.ds(0, 15)], esend.at[0])

    @pl.when(jnp.logical_not(same))
    def _():
        drain(rc.at[0], asend.at[1])
        drain(rc.at[0], esend.at[1])

    drain(lr, lsend)
    drain(wg.at[1], wsend.at[0])
    drain(wu.at[1], wsend.at[1])
    drain(wd.at[pl.ds(HID, HID)], wsend.at[2])
    drain(ga.at[:, pl.ds(1, 15)], gsend)
    drain(rb.at[:, pl.ds(1, 15)], rsend)


def body(
    queries, cache_keys, cache_values, new_keys, new_values, lengths,
    moe_input, router_weight, expert_ids, gate_weight, up_weight, down_weight,
):
    vm = pl.BlockSpec(memory_space=pltpu.VMEM)
    hbm = pl.BlockSpec(memory_space=pltpu.HBM)
    dma = pltpu.SemaphoreType.DMA
    return pl.pallas_call(
        kernel,
        out_shape=(
            jax.ShapeDtypeStruct((1, 768), BF),
            jax.ShapeDtypeStruct((16, W), BF),
        ),
        in_specs=[hbm] * 12,
        out_specs=(vm, vm),
        scratch_shapes=[
            pltpu.VMEM((1, 768), BF),
            pltpu.VMEM((1, 128), BF),
            pltpu.VMEM((1, 128), BF),
            pltpu.VMEM((1, 1), jnp.int32),
            pltpu.VMEM((16, W), BF),
            pltpu.VMEM((8, W), BF),
            pltpu.VMEM((2, 16), jnp.int32),
            pltpu.VMEM((512, 128), BF),
            pltpu.VMEM((512, 128), BF),
            pltpu.VMEM((2, D, HID), BF),
            pltpu.VMEM((2, D, HID), BF),
            pltpu.VMEM((2 * HID, D), BF),
            pltpu.VMEM((8, 16, 128), BF),
            pltpu.VMEM((NG, 16, RAW, 128), BF),
            pltpu.VMEM((4 * BLK, D), BF),
            pltpu.VMEM((4 * BLK, 2 * HID), BF),
            pltpu.VMEM((NG, 16, RAW, 128), BF),
            pltpu.VMEM((NG, 16, RAW, 128), BF),
            pltpu.VMEM((NG, RAW, 128), BF),
            pltpu.VMEM((16, 16, 128), BF),
            pltpu.VMEM((16, 128), F32),
            pltpu.VMEM((7, 16, 128), F32),
            dma((7,)),
            dma((5,)),
            dma((3,)),
            dma((3,)),
            dma((2,)),
            dma((NG,)),
            dma,
            dma((NG,)),
            dma,
            dma((NG,)),
            dma((2,)),
            dma,
            dma,
            dma,
        ],
        compiler_params=pltpu.CompilerParams(
            collective_id=0, has_side_effects=True, vmem_limit_bytes=60 * 1024 * 1024
        ),
        cost_estimate=pl.CostEstimate(flops=1600000000, bytes_accessed=5500000, transcendentals=100000),
    )(
        queries, cache_keys, cache_values, new_keys, new_values, lengths.reshape(1, 1),
        moe_input, router_weight, expert_ids.T, gate_weight, up_weight, down_weight,
    )


def solution(mesh):
    placed = (
        P(("attn", "exp"), "tp"),
        P(("attn", "exp"), None, "tp"),
        P(("attn", "exp"), None, "tp"),
        P(("attn", "exp"), "tp"),
        P(("attn", "exp"), "tp"),
        P(("attn", "exp")),
        P(("attn", "exp"), "tp"),
        P(None, "tp"),
        P(("attn", "exp"), None),
        P("exp", None, ("attn", "tp")),
        P("exp", None, ("attn", "tp")),
        P("exp", ("attn", "tp"), None),
    )
    return jax.shard_map(
        body,
        mesh=mesh,
        in_specs=placed,
        out_specs=(P(("attn", "exp"), "tp"), P(("attn", "exp"), "tp")),
        check_vma=False,
    )
```

```python
import math

import jax
import jax.numpy as jnp
from jax import lax
from jax.experimental import pallas as pl
from jax.experimental.pallas import tpu as pltpu
from jax.sharding import PartitionSpec as P

MESH = pl.DeviceIdType.MESH
BF = jnp.bfloat16
F32 = jnp.float32
NT = 8
W = 384
NG = 4
GS = 8 // NG
RAW = 32 * GS
BLK = 8 * GS
STEPS = ((2, 1, 3, 0),)
SPREAD = (0, 1, 3, 2)
WORK = (0, 1, 3, 2)
LATE = (0,)
BACK = (1, 3, 2, 0)
NEAR = (0, 1, -1, 2, -2, 3, -3, 4)
PLANE = ((2, 2), (1, 2), (2, 1), (3, 2), (2, 3), (0, 2), (2, 0), (1, 1), (3, 3), (1, 3), (3, 1), (0, 1), (1, 0), (0, 3), (3, 0))
HID = 256
D = 3072


def iota(shape, dim):
    return lax.broadcasted_iota(jnp.int32, shape, dim)


def chunk_of(m):
    return (m >= 5).astype(jnp.int32) + (m >= 10).astype(jnp.int32) + (m >= 15).astype(jnp.int32)


def dot(a, b):
    return jnp.dot(a, b, preferred_element_type=F32)


def drain(ref, sem):
    pltpu.make_async_copy(ref, ref, sem).wait()


def attention(q_ref, ck, cv, nk_ref, nv_ref, len_ref, att_ref):
    scale = 1.0 / math.sqrt(128)
    q = q_ref[...]
    heads = [q[:, h * 128 : (h + 1) * 128] for h in range(6)]
    qh = jnp.concatenate(heads + [jnp.zeros((2, 128), BF)], axis=0)
    scores = lax.dot_general(qh, ck[...], (((1,), (1,)), ((), ())), preferred_element_type=F32) * scale
    own = jnp.sum(qh.astype(F32) * nk_ref[...].astype(F32), axis=1, keepdims=True) * scale
    visible = iota(scores.shape, 1) < len_ref[...]
    scores = jnp.where(visible, scores, -jnp.inf)
    peak = jnp.maximum(jnp.max(scores, axis=1, keepdims=True), own)
    weights = jnp.exp(scores - peak)
    own_weight = jnp.exp(own - peak)
    total = jnp.sum(weights, axis=1, keepdims=True) + own_weight
    probs = (weights / total).astype(BF)
    own_prob = (own_weight / total).astype(BF).astype(F32)
    result = dot(probs, cv[...]) + own_prob * nv_ref[...].astype(F32)
    result = result.astype(BF)
    for h in range(6):
        att_ref[:, h * 128 : (h + 1) * 128] = result[h : h + 1, :]


def kernel(
    q_hbm, ck_hbm, cv_hbm, nk_hbm, nv_hbm, len_hbm, x_hbm, rw_hbm, ids_hbm, gate_hbm, up_hbm, down_hbm,
    att_ref, out_ref,
    q_ref, nk_ref, nv_ref, len_ref, x_ref, rw_ref, ids_ref, ck, cv, wg, wu, wd,
    pk, ga, lhs, hid, sb, rb, pe, rc, lp, lr,
    small_sem, loc_sem, wsend, wrecv, asend, arecv, gsend, grecv, rsend, rrecv, esend, erecv, lsend, lrecv,
):
    x = lax.axis_index("attn")
    t = lax.axis_index("tp")
    z = lax.axis_index("exp")
    y = t // 2
    c = t % 2
    odd = z % 2
    half = 1 - odd
    zi = z // 2
    same = half == c

    def start(src, dst, ssem, rsem, device):
        pltpu.make_async_remote_copy(
            src_ref=src, dst_ref=dst, send_sem=ssem, recv_sem=rsem, device_id=device, device_id_type=MESH
        ).start()

    barrier = pltpu.get_barrier_semaphore()

    def greet(device):
        pl.semaphore_signal(barrier, inc=1, device_id=device, device_id_type=MESH)

    turn = jnp.where((c == 0) & (odd == 0), -1, 1)
    source = [2 * ((zi + turn * NEAR[p] + 8) % 8) + 1 - c for p in range(8)]

    for p in reversed(range(8)):
        greet((x, 2 * y + 1 - c, source[p]))
        if p:
            greet((x, t, source[p]))

    @pl.when(jnp.logical_not(same))
    def _():
        greet((x, t, source[0]))

    for dx, dy in PLANE:
        greet(((x + dx) % 4, 2 * ((y + dy) % 4) + c, z))
    for dt in range(1, NT):
        greet((x, (t + dt) % NT, z))

    small = [
        pltpu.make_async_copy(src, dst, small_sem.at[i])
        for i, (src, dst) in enumerate([
            (ids_hbm, ids_ref), (x_hbm, x_ref), (rw_hbm, rw_ref), (q_hbm, q_ref),
            (nk_hbm, nk_ref), (nv_hbm, nv_ref), (len_hbm, len_ref),
        ])
    ]
    large = [
        pltpu.make_async_copy(ck_hbm.at[0], ck, loc_sem.at[0]),
        pltpu.make_async_copy(cv_hbm.at[0], cv, loc_sem.at[1]),
        pltpu.make_async_copy(gate_hbm.at[0], wg.at[0], loc_sem.at[2]),
        pltpu.make_async_copy(up_hbm.at[0], wu.at[0], loc_sem.at[3]),
        pltpu.make_async_copy(down_hbm.at[0], wd.at[pl.ds(0, HID)], loc_sem.at[4]),
    ]
    for copy in small:
        copy.start()
    for copy in large:
        copy.start()

    small[0].wait()
    ids = ids_ref[...]
    row = [ids[0:1, :], ids[1:2, :]]
    eye = iota((16, 16), 0) == iota((16, 16), 1)
    col = [jnp.sum(jnp.where(eye, r, 0), axis=1, keepdims=True) for r in row]
    low = iota((16, 16), 0) < iota((16, 16), 1)
    high = iota((16, 16), 1) < iota((16, 16), 0)

    def count(mask, axis):
        return jnp.sum(mask.astype(jnp.int32), axis=axis, keepdims=True)

    same00, same11 = col[0] == row[0], col[1] == row[1]
    slot_row = [
        count(same00 & low, 0),
        count(col[0] == row[1], 0) + count(same11 & low, 0),
    ]
    slot_col = [
        count(same00 & high, 1),
        count(col[1] == row[0], 1) + count(same11 & high, 1),
    ]

    place = iota((128, 16), 0)
    expert, m = place >> 4, place & 15
    chunk = chunk_of(m)
    slot = m - 5 * chunk
    taken = ((row[0] == expert) & (slot_row[0] == slot)) | ((row[1] == expert) & (slot_row[1] == slot))
    packed = jnp.zeros((128, 128), F32)
    small[1].wait()
    for k in range(3):
        mat = jnp.where(taken & (chunk == k), 1.0, 0.0).astype(BF)
        packed = packed + dot(mat, x_ref[:, k * 128 : (k + 1) * 128])
    pk[...] = packed.astype(BF).reshape(8, 16, 128)

    small[2].wait()
    logits = lax.dot_general(x_ref[...], rw_ref[...], (((1,), (1,)), ((), ())), preferred_element_type=F32)
    lp[...] = jnp.zeros((16, 128), F32)
    lp[:, 0:8] = logits

    pl.semaphore_wait(barrier, 15 + 7 + 15 + jnp.where(same, 0, 1))

    def spot(p):
        return ga.at[p // GS, 0, pl.ds(pl.multiple_of(16 * (2 * (p % GS) + c), 16), 16)]

    for p in reversed(range(8)):
        for b in range(2):
            sign = jnp.where((odd == 1) & (b == 0), -1, 1)
            target = (zi - sign * NEAR[p] + 8) % 8
            if p:
                start(pk.at[target], spot(p), asend.at[0], arecv.at[p // GS], (x, 2 * y + half, 2 * target + b))
            else:
                @pl.when(odd != b)
                def _(target=target, b=b):
                    start(pk.at[target], spot(0), asend.at[0], arecv.at[0], (x, 2 * y + half, 2 * target + b))

    @pl.when(same)
    def _():
        pltpu.make_async_copy(pk.at[zi], spot(0), arecv.at[0]).start()

    @pl.when(jnp.logical_not(same))
    def _():
        start(pk.at[zi], spot(0), asend.at[1], arecv.at[0], (x, 2 * y + half, z))

    sibling = (x, 2 * y + 1 - c, z)
    start(gate_hbm.at[0], wg.at[1], wsend.at[0], wrecv.at[0], sibling)
    start(up_hbm.at[0], wu.at[1], wsend.at[1], wrecv.at[1], sibling)
    start(down_hbm.at[0], wd.at[pl.ds(HID, HID)], wsend.at[2], wrecv.at[2], sibling)

    for dt in range(1, NT):
        start(lp, lr.at[dt - 1], lsend, lrecv, (x, (t + dt) % NT, z))

    for copy in small[3:]:
        copy.wait()
    large[0].wait()
    large[1].wait()
    attention(q_ref, ck, cv, nk_ref, nv_ref, len_ref, att_ref)

    for g in SPREAD:
        drain(ga.at[g, 0], arecv.at[g])
        for dx, dy in PLANE:
            start(
                ga.at[g, 0], ga.at[g, 4 * dy + dx], gsend, grecv.at[g],
                ((x + dx) % 4, 2 * ((y + dy) % 4) + c, z),
            )

    for copy in large[2:]:
        copy.wait()
    drain(wg.at[1], wrecv.at[0])
    drain(wu.at[1], wrecv.at[1])
    drain(wd.at[pl.ds(HID, HID)], wrecv.at[2])

    def piece_row(raw):
        m = raw & 15
        chunk = chunk_of(m)
        inner = (raw >> 5) * 5 + m - 5 * chunk
        return jnp.where(chunk == 3, -1, (((raw >> 4) & 1) * 3 + chunk) * BLK + inner)

    pieces = 6 * BLK
    unpack = jnp.where(piece_row(iota((pieces, RAW), 1)) == iota((pieces, RAW), 0), 1.0, 0.0).astype(BF)
    repack = jnp.where(piece_row(iota((RAW, pieces), 0)) == iota((RAW, pieces), 1), 1.0, 0.0).astype(BF)

    def compute(g, send):
        for dy in range(4):
            raw = jnp.concatenate([ga[g, 4 * dy + dx] for dx in range(4)], axis=1)
            rows = dot(unpack, raw).astype(BF)
            for dx in range(4):
                for k in range(6):
                    lhs[dx * BLK : (dx + 1) * BLK, dy * 768 + k * 128 : dy * 768 + (k + 1) * 128] = rows[
                        k * BLK : (k + 1) * BLK, dx * 128 : (dx + 1) * 128
                    ]
        for h in range(2):
            gate = jnp.zeros((4 * BLK, HID), F32)
            up = jnp.zeros((4 * BLK, HID), F32)
            for dy in range(4):
                a = lhs[:, dy * 768 : (dy + 1) * 768]
                features = pl.ds(pl.multiple_of(((y + 4 - dy) % 4) * 768, 768), 768)
                gate = gate + dot(a, wg[h, features, :])
                up = up + dot(a, wu[h, features, :])
            hid[:, h * HID : (h + 1) * HID] = (gate / (1.0 + jnp.exp(-gate)) * up).astype(BF)
        blocks = [(4 - dx) % 4 for dx in range(4)]
        for step in STEPS:
            terms = []
            for dy in step:
                features = pl.ds(pl.multiple_of(((y + dy) % 4) * 768, 768), 768)
                terms.append(dot(hid[...], wd[:, features]).astype(BF))
            for dy, term in zip(step, terms):
                stacked = jnp.concatenate(
                    [
                        jnp.concatenate([term[b * BLK : (b + 1) * BLK, k * 128 : (k + 1) * 128] for b in blocks], axis=1)
                        for k in range(6)
                    ],
                    axis=0,
                )
                back = dot(repack, stacked).astype(BF)
                for dx in range(4):
                    sb[g, 4 * dy + dx] = back[:, dx * 128 : (dx + 1) * 128]
            if send:
                send_sums(g)

    def send_sums(g):
        for dx, dy in PLANE:
            start(
                sb.at[g, 4 * dy + dx], rb.at[g, 4 * dy + dx], rsend, rrecv.at[g],
                ((x + dx) % 4, 2 * ((y + dy) % 4) + c, z),
            )

    for g in WORK:
        drain(ga.at[g, pl.ds(1, 15)], grecv.at[g])
        compute(g, g not in LATE)
    for g in LATE:
        send_sums(g)

    for g in BACK:
        drain(rb.at[g, pl.ds(1, 15)], rrecv.at[g])
        total = sb[g, 0].astype(F32)
        for i in range(1, 16):
            total = total + rb[g, i].astype(F32)
        pe[g] = total.astype(BF)
        for q in range(GS):
            p = g * GS + q
            for b in range(2):
                ct = (c + b) % 2
                message = pe.at[g, pl.ds(pl.multiple_of(16 * (2 * q + ct), 16), 16)]
                if p or b:
                    start(message, rc.at[z], esend.at[0], erecv, (x, 2 * y + ct, source[p]))
                else:
                    @pl.when(same)
                    def _(message=message):
                        pltpu.make_async_copy(message, rc.at[z], erecv).start()

                    @pl.when(jnp.logical_not(same))
                    def _(message=message):
                        start(message, rc.at[z], esend.at[1], erecv, (x, t, source[0]))

    drain(lr, lrecv)
    full = lp[...]
    for dt in range(NT - 1):
        full = full + lr[dt]
    lane = iota((16, 128), 1)
    chosen = [jnp.sum(jnp.where(lane == col[k], full, 0.0), axis=1, keepdims=True) for k in range(2)]
    mixing = [1.0 / (1.0 + jnp.exp(chosen[1 - k] - chosen[k])) for k in range(2)]

    place = iota((16, 256), 1)
    m = place & 15
    chunk = chunk_of(m)
    slot = m - 5 * chunk
    own = [(col[k] == (place >> 5)) & (slot_col[k] == slot) for k in range(2)]
    picks = [[jnp.where(own[j] & (chunk == k), 1.0, 0.0).astype(BF) for j in range(2)] for k in range(3)]
    drain(rc, erecv)
    returned = rc[...].reshape(256, 128)
    for k in range(3):
        value = [dot(picks[k][j], returned) for j in range(2)]
        out_ref[:, k * 128 : (k + 1) * 128] = (mixing[0] * value[0] + mixing[1] * value[1]).astype(BF)

    drain(rc.at[pl.ds(0, 15)], asend.at[0])
    drain(rc.at[pl.ds(0, 15)], esend.at[0])

    @pl.when(jnp.logical_not(same))
    def _():
        drain(rc.at[0], asend.at[1])
        drain(rc.at[0], esend.at[1])

    drain(lr, lsend)
    drain(wg.at[1], wsend.at[0])
    drain(wu.at[1], wsend.at[1])
    drain(wd.at[pl.ds(HID, HID)], wsend.at[2])
    drain(ga.at[:, pl.ds(1, 15)], gsend)
    drain(rb.at[:, pl.ds(1, 15)], rsend)


def body(
    queries, cache_keys, cache_values, new_keys, new_values, lengths,
    moe_input, router_weight, expert_ids, gate_weight, up_weight, down_weight,
):
    vm = pl.BlockSpec(memory_space=pltpu.VMEM)
    hbm = pl.BlockSpec(memory_space=pltpu.HBM)
    dma = pltpu.SemaphoreType.DMA
    return pl.pallas_call(
        kernel,
        out_shape=(
            jax.ShapeDtypeStruct((1, 768), BF),
            jax.ShapeDtypeStruct((16, W), BF),
        ),
        in_specs=[hbm] * 12,
        out_specs=(vm, vm),
        scratch_shapes=[
            pltpu.VMEM((1, 768), BF),
            pltpu.VMEM((1, 128), BF),
            pltpu.VMEM((1, 128), BF),
            pltpu.VMEM((1, 1), jnp.int32),
            pltpu.VMEM((16, W), BF),
            pltpu.VMEM((8, W), BF),
            pltpu.VMEM((2, 16), jnp.int32),
            pltpu.VMEM((512, 128), BF),
            pltpu.VMEM((512, 128), BF),
            pltpu.VMEM((2, D, HID), BF),
            pltpu.VMEM((2, D, HID), BF),
            pltpu.VMEM((2 * HID, D), BF),
            pltpu.VMEM((8, 16, 128), BF),
            pltpu.VMEM((NG, 16, RAW, 128), BF),
            pltpu.VMEM((4 * BLK, D), BF),
            pltpu.VMEM((4 * BLK, 2 * HID), BF),
            pltpu.VMEM((NG, 16, RAW, 128), BF),
            pltpu.VMEM((NG, 16, RAW, 128), BF),
            pltpu.VMEM((NG, RAW, 128), BF),
            pltpu.VMEM((16, 16, 128), BF),
            pltpu.VMEM((16, 128), F32),
            pltpu.VMEM((7, 16, 128), F32),
            dma((7,)),
            dma((5,)),
            dma((3,)),
            dma((3,)),
            dma((2,)),
            dma((NG,)),
            dma,
            dma((NG,)),
            dma,
            dma((NG,)),
            dma((2,)),
            dma,
            dma,
            dma,
        ],
        compiler_params=pltpu.CompilerParams(
            collective_id=0, has_side_effects=True, vmem_limit_bytes=60 * 1024 * 1024
        ),
        cost_estimate=pl.CostEstimate(flops=1600000000, bytes_accessed=5500000, transcendentals=100000),
    )(
        queries, cache_keys, cache_values, new_keys, new_values, lengths.reshape(1, 1),
        moe_input, router_weight, expert_ids.T, gate_weight, up_weight, down_weight,
    )


def solution(mesh):
    placed = (
        P(("attn", "exp"), "tp"),
        P(("attn", "exp"), None, "tp"),
        P(("attn", "exp"), None, "tp"),
        P(("attn", "exp"), "tp"),
        P(("attn", "exp"), "tp"),
        P(("attn", "exp")),
        P(("attn", "exp"), "tp"),
        P(None, "tp"),
        P(("attn", "exp"), None),
        P("exp", None, ("attn", "tp")),
        P("exp", None, ("attn", "tp")),
        P("exp", ("attn", "tp"), None),
    )
    return jax.shard_map(
        body,
        mesh=mesh,
        in_specs=placed,
        out_specs=(P(("attn", "exp"), "tp"), P(("attn", "exp"), "tp")),
        check_vma=False,
    )
```

```python
import math

import jax
import jax.numpy as jnp
from jax import lax
from jax.experimental import pallas as pl
from jax.experimental.pallas import tpu as pltpu
from jax.sharding import PartitionSpec as P

MESH = pl.DeviceIdType.MESH
BF = jnp.bfloat16
F32 = jnp.float32
NT = 8
W = 384
NG = 4
GS = 8 // NG
RAW = 32 * GS
BLK = 8 * GS
STEPS = ((2, 1, 3, 0),)
SPREAD = (0, 1, 3, 2)
WORK = (0, 1, 3, 2)
LATE = (0,)
BACK = (1, 3, 2, 0)
NEAR = (0, 1, -1, 2, -2, 3, -3, 4)
PLANE = ((2, 2), (1, 2), (2, 1), (3, 2), (2, 3), (0, 2), (2, 0), (1, 1), (3, 3), (1, 3), (3, 1), (0, 1), (1, 0), (0, 3), (3, 0))
HID = 256
D = 3072


def iota(shape, dim):
    return lax.broadcasted_iota(jnp.int32, shape, dim)


def chunk_of(m):
    return (m >= 5).astype(jnp.int32) + (m >= 10).astype(jnp.int32) + (m >= 15).astype(jnp.int32)


def dot(a, b):
    return jnp.dot(a, b, preferred_element_type=F32)


def drain(ref, sem):
    pltpu.make_async_copy(ref, ref, sem).wait()


def attention(q_ref, ck, cv, nk_ref, nv_ref, len_ref, att_ref):
    scale = 1.0 / math.sqrt(128)
    q = q_ref[...]
    heads = [q[:, h * 128 : (h + 1) * 128] for h in range(6)]
    qh = jnp.concatenate(heads + [jnp.zeros((2, 128), BF)], axis=0)
    scores = lax.dot_general(qh, ck[...], (((1,), (1,)), ((), ())), preferred_element_type=F32) * scale
    own = jnp.sum(qh.astype(F32) * nk_ref[...].astype(F32), axis=1, keepdims=True) * scale
    visible = iota(scores.shape, 1) < len_ref[...]
    scores = jnp.where(visible, scores, -jnp.inf)
    peak = jnp.maximum(jnp.max(scores, axis=1, keepdims=True), own)
    weights = jnp.exp(scores - peak)
    own_weight = jnp.exp(own - peak)
    total = jnp.sum(weights, axis=1, keepdims=True) + own_weight
    probs = (weights / total).astype(BF)
    own_prob = (own_weight / total).astype(BF).astype(F32)
    result = dot(probs, cv[...]) + own_prob * nv_ref[...].astype(F32)
    result = result.astype(BF)
    for h in range(6):
        att_ref[:, h * 128 : (h + 1) * 128] = result[h : h + 1, :]


def kernel(
    q_hbm, ck_hbm, cv_hbm, nk_hbm, nv_hbm, len_hbm, x_hbm, rw_hbm, ids_hbm, gate_hbm, up_hbm, down_hbm,
    att_ref, out_ref,
    q_ref, nk_ref, nv_ref, len_ref, x_ref, rw_ref, ids_ref, ck, cv, wg, wu, wd,
    pk, ga, lhs, hid, sb, rb, pe, rc, lp, lr,
    small_sem, loc_sem, wsend, wrecv, asend, arecv, gsend, grecv, rsend, rrecv, esend, erecv, lsend, lrecv,
):
    x = lax.axis_index("attn")
    t = lax.axis_index("tp")
    z = lax.axis_index("exp")
    y = t // 2
    c = t % 2
    odd = z % 2
    half = 1 - odd
    zi = z // 2
    same = half == c

    def start(src, dst, ssem, rsem, device):
        pltpu.make_async_remote_copy(
            src_ref=src, dst_ref=dst, send_sem=ssem, recv_sem=rsem, device_id=device, device_id_type=MESH
        ).start()

    barrier = pltpu.get_barrier_semaphore()

    def greet(device):
        pl.semaphore_signal(barrier, inc=1, device_id=device, device_id_type=MESH)

    turn = jnp.where((c == 0) & (odd == 0), -1, 1)
    source = [2 * ((zi + turn * NEAR[p] + 8) % 8) + 1 - c for p in range(8)]

    for p in reversed(range(8)):
        greet((x, 2 * y + 1 - c, source[p]))
        if p:
            greet((x, t, source[p]))

    @pl.when(jnp.logical_not(same))
    def _():
        greet((x, t, source[0]))

    for dx, dy in PLANE:
        greet(((x + dx) % 4, 2 * ((y + dy) % 4) + c, z))
    for dt in range(1, NT):
        greet((x, (t + dt) % NT, z))

    small = [
        pltpu.make_async_copy(src, dst, small_sem.at[i])
        for i, (src, dst) in enumerate([
            (ids_hbm, ids_ref), (x_hbm, x_ref), (rw_hbm, rw_ref), (q_hbm, q_ref),
            (nk_hbm, nk_ref), (nv_hbm, nv_ref), (len_hbm, len_ref),
        ])
    ]
    large = [
        pltpu.make_async_copy(ck_hbm.at[0], ck, loc_sem.at[0]),
        pltpu.make_async_copy(cv_hbm.at[0], cv, loc_sem.at[1]),
        pltpu.make_async_copy(gate_hbm.at[0], wg.at[0], loc_sem.at[2]),
        pltpu.make_async_copy(up_hbm.at[0], wu.at[0], loc_sem.at[3]),
        pltpu.make_async_copy(down_hbm.at[0], wd.at[pl.ds(0, HID)], loc_sem.at[4]),
    ]
    for copy in small:
        copy.start()
    for copy in large:
        copy.start()

    small[0].wait()
    ids = ids_ref[...]
    row = [ids[0:1, :], ids[1:2, :]]
    eye = iota((16, 16), 0) == iota((16, 16), 1)
    col = [jnp.sum(jnp.where(eye, r, 0), axis=1, keepdims=True) for r in row]
    low = iota((16, 16), 0) < iota((16, 16), 1)
    high = iota((16, 16), 1) < iota((16, 16), 0)

    def count(mask, axis):
        return jnp.sum(mask.astype(jnp.int32), axis=axis, keepdims=True)

    same00, same11 = col[0] == row[0], col[1] == row[1]
    slot_row = [
        count(same00 & low, 0),
        count(col[0] == row[1], 0) + count(same11 & low, 0),
    ]
    slot_col = [
        count(same00 & high, 1),
        count(col[1] == row[0], 1) + count(same11 & high, 1),
    ]

    place = iota((128, 16), 0)
    expert, m = place >> 4, place & 15
    chunk = chunk_of(m)
    slot = m - 5 * chunk
    taken = ((row[0] == expert) & (slot_row[0] == slot)) | ((row[1] == expert) & (slot_row[1] == slot))
    packed = jnp.zeros((128, 128), F32)
    small[1].wait()
    for k in range(3):
        mat = jnp.where(taken & (chunk == k), 1.0, 0.0).astype(BF)
        packed = packed + dot(mat, x_ref[:, k * 128 : (k + 1) * 128])
    pk[...] = packed.astype(BF).reshape(8, 16, 128)

    small[2].wait()
    logits = lax.dot_general(x_ref[...], rw_ref[...], (((1,), (1,)), ((), ())), preferred_element_type=F32)
    lp[...] = jnp.zeros((16, 128), F32)
    lp[:, 0:8] = logits

    pl.semaphore_wait(barrier, 15 + 7 + 15 + jnp.where(same, 0, 1))

    def spot(p):
        return ga.at[p // GS, 0, pl.ds(pl.multiple_of(16 * (2 * (p % GS) + c), 16), 16)]

    for p in reversed(range(8)):
        for b in range(2):
            sign = jnp.where((odd == 1) & (b == 0), -1, 1)
            target = (zi - sign * NEAR[p] + 8) % 8
            if p:
                start(pk.at[target], spot(p), asend.at[0], arecv.at[p // GS], (x, 2 * y + half, 2 * target + b))
            else:
                @pl.when(odd != b)
                def _(target=target, b=b):
                    start(pk.at[target], spot(0), asend.at[0], arecv.at[0], (x, 2 * y + half, 2 * target + b))

    @pl.when(same)
    def _():
        pltpu.make_async_copy(pk.at[zi], spot(0), arecv.at[0]).start()

    @pl.when(jnp.logical_not(same))
    def _():
        start(pk.at[zi], spot(0), asend.at[1], arecv.at[0], (x, 2 * y + half, z))

    sibling = (x, 2 * y + 1 - c, z)
    start(gate_hbm.at[0], wg.at[1], wsend.at[0], wrecv.at[0], sibling)
    start(up_hbm.at[0], wu.at[1], wsend.at[1], wrecv.at[1], sibling)
    start(down_hbm.at[0], wd.at[pl.ds(HID, HID)], wsend.at[2], wrecv.at[2], sibling)

    for dt in range(1, NT):
        start(lp, lr.at[dt - 1], lsend, lrecv, (x, (t + dt) % NT, z))

    for copy in small[3:]:
        copy.wait()
    large[0].wait()
    large[1].wait()
    attention(q_ref, ck, cv, nk_ref, nv_ref, len_ref, att_ref)

    for g in SPREAD:
        drain(ga.at[g, 0], arecv.at[g])
        for dx, dy in PLANE:
            start(
                ga.at[g, 0], ga.at[g, 4 * dy + dx], gsend, grecv.at[g, dy],
                ((x + dx) % 4, 2 * ((y + dy) % 4) + c, z),
            )

    for copy in large[2:]:
        copy.wait()
    drain(wg.at[1], wrecv.at[0])
    drain(wu.at[1], wrecv.at[1])
    drain(wd.at[pl.ds(HID, HID)], wrecv.at[2])

    def piece_row(raw):
        m = raw & 15
        chunk = chunk_of(m)
        inner = (raw >> 5) * 5 + m - 5 * chunk
        return jnp.where(chunk == 3, -1, (((raw >> 4) & 1) * 3 + chunk) * BLK + inner)

    pieces = 6 * BLK
    unpack = jnp.where(piece_row(iota((pieces, RAW), 1)) == iota((pieces, RAW), 0), 1.0, 0.0).astype(BF)
    repack = jnp.where(piece_row(iota((RAW, pieces), 0)) == iota((RAW, pieces), 1), 1.0, 0.0).astype(BF)

    def arrive(g, dy):
        drain(ga.at[g, pl.ds(4 * dy, 4) if dy else pl.ds(1, 3)], grecv.at[g, dy])

    def unpack_rows(g, dy):
        raw = jnp.concatenate([ga[g, 4 * dy + dx] for dx in range(4)], axis=1)
        rows = dot(unpack, raw).astype(BF)
        for dx in range(4):
            for k in range(6):
                lhs[dx * BLK : (dx + 1) * BLK, dy * 768 + k * 128 : dy * 768 + (k + 1) * 128] = rows[
                    k * BLK : (k + 1) * BLK, dx * 128 : (dx + 1) * 128
                ]

    def add_products(sums, dy):
        a = lhs[:, dy * 768 : (dy + 1) * 768]
        features = pl.ds(pl.multiple_of(((y + 4 - dy) % 4) * 768, 768), 768)
        return [
            sums[2 * h + i] + dot(a, w[h, features, :])
            for h in range(2)
            for i, w in enumerate((wg, wu))
        ]

    def compute(g, send):
        sums = [jnp.zeros((4 * BLK, HID), F32)] * 4
        if g == 3:
            for dy in (0, 1, 3, 2):
                arrive(g, dy)
                unpack_rows(g, dy)
                sums = add_products(sums, dy)
        else:
            for dy in range(4):
                arrive(g, dy)
            for dy in range(4):
                unpack_rows(g, dy)
            for dy in range(4):
                sums = add_products(sums, dy)
        for h in range(2):
            gate, up = sums[2 * h], sums[2 * h + 1]
            hid[:, h * HID : (h + 1) * HID] = (gate / (1.0 + jnp.exp(-gate)) * up).astype(BF)
        blocks = [(4 - dx) % 4 for dx in range(4)]
        for step in STEPS:
            terms = []
            for dy in step:
                features = pl.ds(pl.multiple_of(((y + dy) % 4) * 768, 768), 768)
                terms.append(dot(hid[...], wd[:, features]).astype(BF))
            for dy, term in zip(step, terms):
                stacked = jnp.concatenate(
                    [
                        jnp.concatenate([term[b * BLK : (b + 1) * BLK, k * 128 : (k + 1) * 128] for b in blocks], axis=1)
                        for k in range(6)
                    ],
                    axis=0,
                )
                back = dot(repack, stacked).astype(BF)
                for dx in range(4):
                    sb[g, 4 * dy + dx] = back[:, dx * 128 : (dx + 1) * 128]
            if send:
                send_sums(g)

    def send_sums(g):
        for dx, dy in PLANE:
            start(
                sb.at[g, 4 * dy + dx], rb.at[g, 4 * dy + dx], rsend, rrecv.at[g],
                ((x + dx) % 4, 2 * ((y + dy) % 4) + c, z),
            )

    for g in WORK:
        compute(g, g not in LATE)
    for g in LATE:
        send_sums(g)

    for g in BACK:
        drain(rb.at[g, pl.ds(1, 15)], rrecv.at[g])
        total = sb[g, 0].astype(F32)
        for i in range(1, 16):
            total = total + rb[g, i].astype(F32)
        pe[g] = total.astype(BF)
        for q in range(GS):
            p = g * GS + q
            for b in range(2):
                ct = (c + b) % 2
                message = pe.at[g, pl.ds(pl.multiple_of(16 * (2 * q + ct), 16), 16)]
                if p or b:
                    start(message, rc.at[z], esend.at[0], erecv, (x, 2 * y + ct, source[p]))
                else:
                    @pl.when(same)
                    def _(message=message):
                        pltpu.make_async_copy(message, rc.at[z], erecv).start()

                    @pl.when(jnp.logical_not(same))
                    def _(message=message):
                        start(message, rc.at[z], esend.at[1], erecv, (x, t, source[0]))

    drain(lr, lrecv)
    full = lp[...]
    for dt in range(NT - 1):
        full = full + lr[dt]
    lane = iota((16, 128), 1)
    chosen = [jnp.sum(jnp.where(lane == col[k], full, 0.0), axis=1, keepdims=True) for k in range(2)]
    mixing = [1.0 / (1.0 + jnp.exp(chosen[1 - k] - chosen[k])) for k in range(2)]

    place = iota((16, 256), 1)
    m = place & 15
    chunk = chunk_of(m)
    slot = m - 5 * chunk
    own = [(col[k] == (place >> 5)) & (slot_col[k] == slot) for k in range(2)]
    picks = [[jnp.where(own[j] & (chunk == k), 1.0, 0.0).astype(BF) for j in range(2)] for k in range(3)]
    drain(rc, erecv)
    returned = rc[...].reshape(256, 128)
    for k in range(3):
        value = [dot(picks[k][j], returned) for j in range(2)]
        out_ref[:, k * 128 : (k + 1) * 128] = (mixing[0] * value[0] + mixing[1] * value[1]).astype(BF)

    drain(rc.at[pl.ds(0, 15)], asend.at[0])
    drain(rc.at[pl.ds(0, 15)], esend.at[0])

    @pl.when(jnp.logical_not(same))
    def _():
        drain(rc.at[0], asend.at[1])
        drain(rc.at[0], esend.at[1])

    drain(lr, lsend)
    drain(wg.at[1], wsend.at[0])
    drain(wu.at[1], wsend.at[1])
    drain(wd.at[pl.ds(HID, HID)], wsend.at[2])
    drain(ga.at[:, pl.ds(1, 15)], gsend)
    drain(rb.at[:, pl.ds(1, 15)], rsend)


def body(
    queries, cache_keys, cache_values, new_keys, new_values, lengths,
    moe_input, router_weight, expert_ids, gate_weight, up_weight, down_weight,
):
    vm = pl.BlockSpec(memory_space=pltpu.VMEM)
    hbm = pl.BlockSpec(memory_space=pltpu.HBM)
    dma = pltpu.SemaphoreType.DMA
    return pl.pallas_call(
        kernel,
        out_shape=(
            jax.ShapeDtypeStruct((1, 768), BF),
            jax.ShapeDtypeStruct((16, W), BF),
        ),
        in_specs=[hbm] * 12,
        out_specs=(vm, vm),
        scratch_shapes=[
            pltpu.VMEM((1, 768), BF),
            pltpu.VMEM((1, 128), BF),
            pltpu.VMEM((1, 128), BF),
            pltpu.VMEM((1, 1), jnp.int32),
            pltpu.VMEM((16, W), BF),
            pltpu.VMEM((8, W), BF),
            pltpu.VMEM((2, 16), jnp.int32),
            pltpu.VMEM((512, 128), BF),
            pltpu.VMEM((512, 128), BF),
            pltpu.VMEM((2, D, HID), BF),
            pltpu.VMEM((2, D, HID), BF),
            pltpu.VMEM((2 * HID, D), BF),
            pltpu.VMEM((8, 16, 128), BF),
            pltpu.VMEM((NG, 16, RAW, 128), BF),
            pltpu.VMEM((4 * BLK, D), BF),
            pltpu.VMEM((4 * BLK, 2 * HID), BF),
            pltpu.VMEM((NG, 16, RAW, 128), BF),
            pltpu.VMEM((NG, 16, RAW, 128), BF),
            pltpu.VMEM((NG, RAW, 128), BF),
            pltpu.VMEM((16, 16, 128), BF),
            pltpu.VMEM((16, 128), F32),
            pltpu.VMEM((7, 16, 128), F32),
            dma((7,)),
            dma((5,)),
            dma((3,)),
            dma((3,)),
            dma((2,)),
            dma((NG,)),
            dma,
            dma((NG, 4)),
            dma,
            dma((NG,)),
            dma((2,)),
            dma,
            dma,
            dma,
        ],
        compiler_params=pltpu.CompilerParams(
            collective_id=0, has_side_effects=True, vmem_limit_bytes=60 * 1024 * 1024
        ),
        cost_estimate=pl.CostEstimate(flops=1600000000, bytes_accessed=5500000, transcendentals=100000),
    )(
        queries, cache_keys, cache_values, new_keys, new_values, lengths.reshape(1, 1),
        moe_input, router_weight, expert_ids.T, gate_weight, up_weight, down_weight,
    )


def solution(mesh):
    placed = (
        P(("attn", "exp"), "tp"),
        P(("attn", "exp"), None, "tp"),
        P(("attn", "exp"), None, "tp"),
        P(("attn", "exp"), "tp"),
        P(("attn", "exp"), "tp"),
        P(("attn", "exp")),
        P(("attn", "exp"), "tp"),
        P(None, "tp"),
        P(("attn", "exp"), None),
        P("exp", None, ("attn", "tp")),
        P("exp", None, ("attn", "tp")),
        P("exp", ("attn", "tp"), None),
    )
    return jax.shard_map(
        body,
        mesh=mesh,
        in_specs=placed,
        out_specs=(P(("attn", "exp"), "tp"), P(("attn", "exp"), "tp")),
        check_vma=False,
    )
```
